256 devices in a mesh: row: 8 (over y, x_hi), col: 32 (over z, x_lo, core).
Axes of the slice: x: 4 (x_hi: 2, x_lo: 2; x = x_hi * 2 + x_lo), y: 4, z: 8, core: 2. Of those that a mesh axis runs over, the one named last changes fastest.
Arguments:
- ancestor: float32 [2, 4096, 4096], P(None, 'row', 'col')
- panel: float32 [2, 4096, 512], P(None, 'col'), may hold values from -0.75 to 0.75
- factor_inv: float32 [2, 512, 512], P(None, 'row'), as said below
- pattern: int32 [2, 16], replicated, may hold values from 0 to 15, each once within a row
Outputs:
- column_block: float32 [2, 4096, 512], P(None, ('row', 'col'))
- diagonal_inv: float32 [2, 512], replicated
The draws below stay inside these ranges and needn't reach their ends.
Inputs may be any that keep to these rules, and one draw needn't show every extreme that they name: `pattern`: each row names each of the 16 tile positions exactly once. `factor_inv`: each block is lower triangular with its diagonal between 0.5 and 2.
All inputs are finite; a program needn't handle non-finite values.
Results may differ from the reference program's by a relative error of at most 0.0001.
Values sent between devices are 32-bit elements; how exact they have to be, the bound alone decides.
A program may use at most 64 MiB of HBM per device.

```python
import math
import jax
import jax.numpy as jnp
from jax import lax

B = 256
W = 512
S = 2
R = 16
RB = 4096


def draw_ancestor(key, part):
    key = jax.random.fold_in(key, 11)
    first_key, second_key = jax.random.split(key)
    noise = jax.random.normal(first_key, (S, RB, RB), jnp.float32)
    offdiag = (noise + jnp.swapaxes(noise, 1, 2)) * (0.5 / math.sqrt(RB))
    levels = jnp.exp(jax.random.uniform(second_key, (S, RB), jnp.float32, math.log(0.5), math.log(2.0)))
    rows_idx = jnp.arange(RB, dtype=jnp.int32)
    on_diag = rows_idx[:, None] == rows_idx[None, :]
    return jnp.where(on_diag[None], offdiag + levels[:, :, None], offdiag)


def draw_factor_inv(key, part):
    key = jax.random.fold_in(key, 12)
    first_key, second_key = jax.random.split(key)
    noise = jax.random.normal(first_key, (S, W, W), jnp.float32)
    levels = jnp.exp(jax.random.uniform(second_key, (S, W), jnp.float32, math.log(0.5), math.log(2.0)))
    rows_idx = jnp.arange(W, dtype=jnp.int32)
    below = rows_idx[:, None] > rows_idx[None, :]
    on_diag = rows_idx[:, None] == rows_idx[None, :]
    lower = jnp.where(below[None], noise / math.sqrt(W), 0.0)
    return jnp.where(on_diag[None], levels[:, :, None], lower).astype(jnp.float32)


def block_scale(stream_key, dims, cuts, low, largest):
    level = 1.0
    for dim, parts in cuts:
        heights = jax.random.uniform(jax.random.fold_in(jax.random.fold_in(stream_key, 6), dim), (parts,), jnp.float32, low / len(cuts), largest / len(cuts))
        level = level * jnp.repeat(jnp.exp(heights), dims[dim] // parts).reshape((-1,) + (1,) * (len(dims) - 1 - dim))
    return level


def scatter_about(own_key, shape, width, bound, cuts=(), kind=jnp.bfloat16):
    entries = width * jax.random.normal(own_key, shape, jnp.float32)
    if cuts:
        entries = entries * block_scale(own_key, shape, cuts, -0.22, 0.18)
    return jnp.clip(entries, -bound, bound).astype(kind)


def setup_inputs(seed: int = 0) -> dict:
    seeds = jax.random.split(jax.random.key(seed), 5)
    return {
        "ancestor": draw_ancestor(jax.random.fold_in(seeds[4], 71), 0),
        "panel": scatter_about(seeds[1], (S, RB, W), (B // 4) ** -0.5, 0.75, ((1, 32),), jnp.float32),
        "factor_inv": draw_factor_inv(jax.random.fold_in(seeds[4], 71), 0),
        "pattern": jax.vmap(lambda own: jax.random.permutation(own, R))(jax.random.split(seeds[3], S)).reshape((S, R)).astype(jnp.int32),
    }


def reference(ancestor, panel, factor_inv, pattern):
    highest = lax.Precision.HIGHEST
    scaled_panel = jnp.einsum('srw,swv->srv', panel, factor_inv, precision=highest)
    tiles_view = scaled_panel.reshape(S, R, B, W)
    blocks = jnp.arange(R, dtype=jnp.int32)
    choose = (pattern[:, :, None] == blocks[None, None, :]).astype(jnp.float32)
    spread = jnp.einsum('srn,srbw->snbw', choose, tiles_view, precision=highest).reshape(S, RB, W)
    product = jnp.einsum('sij,sjw->siw', ancestor, spread, precision=highest)
    column_block = -product
    diagonal_inv = jnp.sum(factor_inv * factor_inv, axis=1) + jnp.sum(spread * product, axis=1)
    return column_block, diagonal_inv
```

```python
import jax
import jax.numpy as jnp
from jax import lax
from jax.experimental import pallas as pl
from jax.experimental.pallas import tpu as pltpu
from jax.sharding import PartitionSpec as P


MESH = pl.DeviceIdType.MESH
F32 = jnp.float32
BF16 = jnp.bfloat16

(
    A_RECV, A_SEND, B_RECV, B_SEND, C_RECV_UP, C_RECV_DOWN, C_RECV_UP2, C_RECV_DOWN2,
    C_SEND_UP, C_SEND_DOWN, C_SEND_UP2, C_SEND_DOWN2, ANC_RECV, ANC_SEND_CORE, ANC_SEND_X0, ANC_SEND_X1,
    F_OWN, F_RECV_UP, F_RECV_DOWN, F_RECV_UP2, F_RECV_DOWN2, F_SEND_UP, F_SEND_DOWN, F_SEND_UP2, F_SEND_DOWN2,
    FX_RECV, FX_SEND, PD_RECV, PD_SEND0, PD_SEND1, Y_RECV, Y_SEND, O_RECV, O_SEND, D1_RECV, D1_SEND, D2_RECV, D2_SEND,
    N_SEMS,
) = range(39)


def halves(x):
    high = x.astype(BF16)
    low = (x - high.astype(F32)).astype(BF16)
    return high, low


def dot3(a_high, a_low, b_high, b_low):
    def dot(a, b):
        return jnp.dot(a, b, preferred_element_type=F32)

    return dot(a_high, b_high) + (dot(a_low, b_high) + dot(a_high, b_low))


def kernel(
    anc, pan, fin, pat, out_block, out_diag,
    inv, buf_a, send_b, pbuf, abuf, fbuf, cbuf, rs_up, rs_down, ysum, ybuf, pdiag, spread, prod, d_send, d1, d1_sum, d2,
    a_high, a_low, f_high, f_low, sem, rs_recv, rs_send,
):
    r = lax.axis_index("row")
    c = lax.axis_index("col")
    y, xh = r // 2, r % 2
    z, xl, k = c // 4, (c // 2) % 2, c % 2
    q = 2 * z + xl
    y_up, y_down = (y + 1) % 4, (y + 3) % 4
    z_up, z_down = (z + 1) % 8, (z + 7) % 8

    def col(z_, xl_, k_):
        return z_ * 4 + xl_ * 2 + k_

    def remote(src, dst, send_sem, recv_sem, row_, col_):
        return pltpu.make_async_remote_copy(
            src_ref=src, dst_ref=dst, send_sem=send_sem, recv_sem=recv_sem, device_id=(row_, col_), device_id_type=MESH
        )

    def wait_bytes(ref, s):
        pltpu.make_async_copy(ref, ref, s).wait()

    def start_either(src, dst, send_sem, recv_sem, row_, col_):
        mine = jnp.logical_and(row_ == r, col_ == c)

        @pl.when(mine)
        def _():
            pltpu.make_async_copy(src, dst, recv_sem).start()

        @pl.when(jnp.logical_not(mine))
        def _():
            remote(src, dst, send_sem, recv_sem, row_, col_).start()

    pd_src_row = 2 * ((z % 2) * 2 + xl) + (z % 4) // 2

    with jax.named_scope("greet"):
        barrier = pltpu.get_barrier_semaphore()

        def greet(row_, col_):
            pl.semaphore_signal(barrier, inc=1, device_id=(row_, col_), device_id_type=MESH)

        def greet_col(j, carry):
            greet(r, (c + j) % 32)
            return carry

        lax.fori_loop(1, 32, greet_col, 0)

        def greet_row(j, carry):
            greet((r + j) % 8, c)
            greet((r + j) % 8, col(z, xl, 1 - k))
            return carry

        lax.fori_loop(1, 8, greet_row, 0)
        greet(2 * y + 1 - xh, col(z, 1 - xl, k))
        for x_src in range(2):
            src_col = col(r, x_src, k)

            @pl.when(jnp.logical_not(jnp.logical_and(pd_src_row == r, src_col == c)))
            def _():
                greet(pd_src_row, src_col)

        others = 31 + 14 + 1
        for t in range(2):
            dst_col = col(4 * t + 2 * xh + y // 2, y % 2, k)
            mine = jnp.logical_and(z == r, dst_col == c)
            others = others + jnp.where(mine, jnp.int32(0), jnp.int32(1))
        pl.semaphore_wait(barrier, others)

    with jax.named_scope("start"):
        def send_a(j, carry):
            zi, xi, s = 4 * k + j // 4, (j // 2) % 2, j % 2
            src = pan.at[
                s, pl.ds(pl.multiple_of(32 * y + 8 * (j // 4), 8), 8), pl.ds(pl.multiple_of(256 * xi, 256), 256)
            ]
            start_either(src, buf_a.at[q], sem.at[A_SEND], sem.at[A_RECV], r, col(zi, xi, s))
            return carry

        lax.fori_loop(0, 16, send_a, 0)

        f_own = pltpu.make_async_copy(fin.at[k], fbuf.at[y, xh], sem.at[F_OWN])
        f_own.start()
        f_up = remote(fin.at[k], fbuf.at[y, xh], sem.at[F_SEND_UP], sem.at[F_RECV_UP], 2 * y_up + xh, c)
        f_down = remote(fin.at[k], fbuf.at[y, xh], sem.at[F_SEND_DOWN], sem.at[F_RECV_DOWN], 2 * y_down + xh, c)
        f_up.start()
        f_down.start()

        quarter = abuf.at[2 * xl + k]
        pltpu.make_async_copy(anc.at[k], quarter, sem.at[ANC_RECV]).start()
        anc_core = remote(anc.at[1 - k], quarter, sem.at[ANC_SEND_CORE], sem.at[ANC_RECV], r, col(z, xl, 1 - k))
        anc_x0 = remote(anc.at[0], quarter, sem.at[ANC_SEND_X0], sem.at[ANC_RECV], r, col(z, 1 - xl, 0))
        anc_x1 = remote(anc.at[1], quarter, sem.at[ANC_SEND_X1], sem.at[ANC_RECV], r, col(z, 1 - xl, 1))
        anc_core.start()
        anc_x0.start()
        anc_x1.start()

        def invert(n, carry):
            total = jnp.int32(0)
            for j in range(16):
                total = jnp.where(pat[k, j] == n, jnp.int32(j), total)
            inv[n] = total
            return carry

        lax.fori_loop(0, 16, invert, 0)

    with jax.named_scope("wait_a"):
        wait_bytes(buf_a, sem.at[A_RECV])

    with jax.named_scope("send_b"):
        b_dst = pbuf.at[:, z // 4, y, pl.ds(pl.multiple_of(8 * (z % 4), 8), 8), :]

        def send_b_to(j, carry):
            zd = (z + j) % 8
            send_b[zd, 0] = buf_a[inv[2 * zd]]
            send_b[zd, 1] = buf_a[inv[2 * zd + 1]]
            remote(send_b.at[zd], b_dst, sem.at[B_SEND], sem.at[B_RECV], r, col(zd, xl, k)).start()
            return carry

        lax.fori_loop(1, 8, send_b_to, 0)
        send_b[z, 0] = buf_a[inv[2 * z]]
        send_b[z, 1] = buf_a[inv[2 * z + 1]]
        pltpu.make_async_copy(send_b.at[z], b_dst, sem.at[B_RECV]).start()

    with jax.named_scope("wait_b"):
        wait_bytes(pbuf.at[:, :, y], sem.at[B_RECV])

    with jax.named_scope("send_c"):
        c_up = remote(
            pbuf.at[:, :, y], pbuf.at[:, :, y], sem.at[C_SEND_UP], sem.at[C_RECV_UP], 2 * y_up + xh, c
        )
        c_down = remote(
            pbuf.at[:, :, y], pbuf.at[:, :, y], sem.at[C_SEND_DOWN], sem.at[C_RECV_DOWN], 2 * y_down + xh, c
        )
        c_up.start()
        c_down.start()
        for t in range(2):
            start_either(
                pbuf.at[t, xh, y], pdiag.at[xl], sem.at[PD_SEND0 + t], sem.at[PD_RECV],
                z, col(4 * t + 2 * xh + y // 2, y % 2, k),
            )

    with jax.named_scope("factor_y"):
        wait_bytes(fbuf.at[y_down, xh], sem.at[F_RECV_UP])
        f_up2 = remote(
            fbuf.at[y_down, xh, pl.ds(0, 32)], fbuf.at[y_down, xh, pl.ds(0, 32)],
            sem.at[F_SEND_UP2], sem.at[F_RECV_UP2], 2 * y_up + xh, c,
        )
        f_up2.start()
        wait_bytes(fbuf.at[y_up, xh], sem.at[F_RECV_DOWN])
        f_down2 = remote(
            fbuf.at[y_up, xh, pl.ds(32, 32)], fbuf.at[y_up, xh, pl.ds(32, 32)],
            sem.at[F_SEND_DOWN2], sem.at[F_RECV_DOWN2], 2 * y_down + xh, c,
        )
        f_down2.start()

    with jax.named_scope("wait_c"):
        wait_bytes(pbuf.at[:, :, y_down], sem.at[C_RECV_UP])
        c_up2 = remote(
            pbuf.at[0, :, y_down], pbuf.at[0, :, y_down], sem.at[C_SEND_UP2], sem.at[C_RECV_UP2], 2 * y_up + xh, c
        )
        c_up2.start()
        wait_bytes(pbuf.at[:, :, y_up], sem.at[C_RECV_DOWN])
        c_down2 = remote(
            pbuf.at[1, :, y_up], pbuf.at[1, :, y_up], sem.at[C_SEND_DOWN2], sem.at[C_RECV_DOWN2], 2 * y_down + xh, c
        )
        c_down2.start()

    with jax.named_scope("factor_x"):
        f_own.wait()
        y_far = (y + 2) % 4
        wait_bytes(fbuf.at[y_far, xh, pl.ds(0, 32)], sem.at[F_RECV_UP2])
        wait_bytes(fbuf.at[y_far, xh, pl.ds(32, 32)], sem.at[F_RECV_DOWN2])
        f_x = remote(
            fbuf.at[:, xh], fbuf.at[:, xh], sem.at[FX_SEND], sem.at[FX_RECV], 2 * y + 1 - xh, col(z, 1 - xl, k)
        )
        f_x.start()

    with jax.named_scope("wait_anc"):
        wait_bytes(abuf, sem.at[ANC_RECV])
        for j in range(4):
            high, low = halves(abuf[j])
            a_high[:, 128 * j : 128 * j + 128] = high
            a_low[:, 128 * j : 128 * j + 128] = low

    with jax.named_scope("wait_c2"):
        wait_bytes(pbuf.at[0, :, y_far], sem.at[C_RECV_UP2])
        wait_bytes(pbuf.at[1, :, y_far], sem.at[C_RECV_DOWN2])

    with jax.named_scope("product"):
        p_high, p_low = halves(pbuf[...].reshape(512, 256))
        cbuf[...] = dot3(a_high[...], a_low[...], p_high, p_low).reshape(8, 64, 256)

    sends = []

    def rs_step(step):
        distance = 4 - step
        for sub in range(2):
            rows = pl.ds(32 * sub, 32)
            for way in range(2):
                buf = (rs_up, rs_down)[way]
                zd = (z + distance) % 8 if way == 0 else (z + 8 - distance) % 8
                to = z_up if way == 0 else z_down
                half = pl.ds(128 * way, 128)
                if step == 0:
                    cols = half
                else:
                    cols = pl.ds(0, 256)
                    before = half if step == 1 else pl.ds(0, 256)
                    wait_bytes(buf.at[step - 1, rows, before], rs_recv.at[way, step - 1, sub])
                    cbuf[zd, rows, before] += buf[step - 1, rows, before]
                copy = remote(
                    cbuf.at[zd, rows, cols], buf.at[step, rows, cols],
                    rs_send.at[way, step, sub], rs_recv.at[way, step, sub], r, col(to, xl, k),
                )
                copy.start()
                sends.append(copy)

    with jax.named_scope("reduce0"):
        rs_step(0)
    with jax.named_scope("reduce1"):
        rs_step(1)
    with jax.named_scope("factor"):
        wait_bytes(fbuf.at[:, 1 - xh], sem.at[FX_RECV])
        factor = fbuf[...].reshape(512, 512)
        high, low = halves(factor)
        f_high[...] = high
        f_low[...] = low
    with jax.named_scope("reduce2"):
        rs_step(2)
    with jax.named_scope("spread"):
        wait_bytes(pdiag, sem.at[PD_RECV])
        s_high, s_low = halves(jnp.concatenate([pdiag[0], pdiag[1]], axis=1))
        spread[...] = dot3(s_high, s_low, f_high[...], f_low[...])
    with jax.named_scope("reduce3"):
        rs_step(3)
    with jax.named_scope("reduce4"):
        for sub in range(2):
            rows = pl.ds(32 * sub, 32)
            for way in range(2):
                wait_bytes((rs_up, rs_down)[way].at[3, rows, :], rs_recv.at[way, 3, sub])
            ysum[sub] = cbuf[z, rows, :] + (rs_up[3, rows, :] + rs_down[3, rows, :])
        y_copy = remote(ysum.at[1 - xl], ybuf.at[xl], sem.at[Y_SEND], sem.at[Y_RECV], r, col(z, 1 - xl, k))
        y_copy.start()
        ybuf[xl] = ysum[xl]
        wait_bytes(ybuf.at[1 - xl], sem.at[Y_RECV])

    with jax.named_scope("apply_factor"):
        y_high, y_low = halves(jnp.concatenate([ybuf[0], ybuf[1]], axis=1))
        result = dot3(y_high, y_low, f_high[...], f_low[...])
        prod[...] = -result.reshape(2, 16, 512)
        o_copy = remote(prod.at[1 - k], out_block.at[k], sem.at[O_SEND], sem.at[O_RECV], r, col(z, xl, 1 - k))
        o_copy.start()
        d_send[...] = jnp.sum(spread[...] * result, axis=0, keepdims=True)
        d1[q] = d_send[...]

    with jax.named_scope("diag_col"):
        def send_d1(j, carry):
            remote(d_send, d1.at[q], sem.at[D1_SEND], sem.at[D1_RECV], r, (c + 2 * j) % 32).start()
            return carry

        lax.fori_loop(1, 16, send_d1, 0)
        out_block[k] = prod[k]
        own_factor = fbuf[y, xh]
        own_sq = jnp.sum(own_factor * own_factor, axis=0, keepdims=True)
        wait_bytes(d1.at[pl.ds(0, 15)], sem.at[D1_RECV])
        d1_sum[...] = jnp.sum(d1[...], axis=0) + own_sq
        d2[k, r] = d1_sum[...]

    with jax.named_scope("diag_row"):
        def send_d2(j, carry):
            remote(d1_sum, d2.at[k, r], sem.at[D2_SEND], sem.at[D2_RECV], (r + j) % 8, c).start()
            remote(d1_sum, d2.at[k, r], sem.at[D2_SEND], sem.at[D2_RECV], (r + j) % 8, col(z, xl, 1 - k)).start()
            return carry

        lax.fori_loop(1, 8, send_d2, 0)
        remote(d1_sum, d2.at[k, r], sem.at[D2_SEND], sem.at[D2_RECV], r, col(z, xl, 1 - k)).start()
        wait_bytes(d1.at[pl.ds(0, 15)], sem.at[D2_RECV])
        for s in range(2):
            out_diag[pl.ds(s, 1), :] = jnp.sum(d2[s], axis=0)

    with jax.named_scope("finish"):
        wait_bytes(out_block.at[1 - k], sem.at[O_RECV])
        for copy in [f_up, f_down, f_up2, f_down2, f_x, anc_core, anc_x0, anc_x1, c_up, c_down, c_up2, c_down2, y_copy, o_copy] + sends:
            copy.wait_send()
        wait_bytes(d1.at[pl.ds(0, 15)], sem.at[D1_SEND])
        wait_bytes(d1.at[pl.ds(0, 15)], sem.at[D2_SEND])
        wait_bytes(send_b.at[pl.ds(0, 7)], sem.at[B_SEND])
        a_self = z // 4 == k

        @pl.when(a_self)
        def _():
            wait_bytes(buf_a.at[pl.ds(0, 15)], sem.at[A_SEND])

        @pl.when(jnp.logical_not(a_self))
        def _():
            wait_bytes(buf_a, sem.at[A_SEND])

        for t in range(2):
            dst_col = col(4 * t + 2 * xh + y // 2, y % 2, k)

            @pl.when(jnp.logical_not(jnp.logical_and(z == r, dst_col == c)))
            def _():
                wait_bytes(pdiag.at[0], sem.at[PD_SEND0 + t])


def per_device(ancestor, panel, factor_inv, pattern):
    vmem = pltpu.VMEM
    return pl.pallas_call(
        kernel,
        out_shape=(jax.ShapeDtypeStruct((2, 16, 512), F32), jax.ShapeDtypeStruct((2, 512), F32)),
        in_specs=[pl.BlockSpec(memory_space=pl.ANY)] * 3 + [pl.BlockSpec(memory_space=pltpu.SMEM)],
        out_specs=(pl.BlockSpec(memory_space=vmem), pl.BlockSpec(memory_space=vmem)),
        scratch_shapes=[
            pltpu.SMEM((16,), jnp.int32),
            vmem((16, 8, 256), F32),
            vmem((8, 2, 8, 256), F32),
            vmem((2, 2, 4, 32, 256), F32),
            vmem((4, 512, 128), F32),
            vmem((4, 2, 64, 512), F32),
            vmem((8, 64, 256), F32),
            vmem((4, 64, 256), F32),
            vmem((4, 64, 256), F32),
            vmem((2, 32, 256), F32),
            vmem((2, 32, 256), F32),
            vmem((2, 32, 256), F32),
            vmem((32, 512), F32),
            vmem((2, 16, 512), F32),
            vmem((1, 512), F32),
            vmem((16, 1, 512), F32),
            vmem((1, 512), F32),
            vmem((2, 8, 1, 512), F32),
            vmem((512, 512), BF16),
            vmem((512, 512), BF16),
            vmem((512, 512), BF16),
            vmem((512, 512), BF16),
            pltpu.SemaphoreType.DMA((N_SEMS,)),
            pltpu.SemaphoreType.DMA((2, 4, 2)),
            pltpu.SemaphoreType.DMA((2, 4, 2)),
        ],
        compiler_params=pltpu.CompilerParams(
            collective_id=0, has_side_effects=True, vmem_limit_bytes=32 * 1024 * 1024
        ),
    )(ancestor, panel, factor_inv, pattern)


def solution(mesh):
    in_specs = (P(None, "row", "col"), P(None, "col", None), P(None, "row", None), P())
    out_specs = (P(None, ("row", "col"), None), P())
    return jax.shard_map(per_device, mesh=mesh, in_specs=in_specs, out_specs=out_specs, check_vma=False)
```

```python
import jax
import jax.numpy as jnp
from jax import lax
from jax.experimental import pallas as pl
from jax.experimental.pallas import tpu as pltpu
from jax.sharding import PartitionSpec as P


MESH = pl.DeviceIdType.MESH
F32 = jnp.float32
BF16 = jnp.bfloat16
STOP = ""


def halves(x):
    high = x.astype(BF16)
    low = (x - high.astype(F32)).astype(BF16)
    return high, low


def dot3(a_high, a_low, b_high, b_low):
    def dot(a, b):
        return jnp.dot(a, b, preferred_element_type=F32)

    return dot(a_high, b_high) + (dot(a_low, b_high) + dot(a_high, b_low))


def kernel(
    anc, pan, fin, pat_hbm, out_block, out_diag,
    pat, inv, buf_a, send_b, pbuf, abuf, fbuf, cbuf, rbuf, pdiag, spread, prod, d_send, own_sq, d1, d1_sum, d2,
    a_high, a_low, f_high, f_low, sems,
):
    r = lax.axis_index("row")
    c = lax.axis_index("col")
    y, xh = r // 2, r % 2
    z, xl, k = c // 4, (c // 2) % 2, c % 2
    q = 2 * z + xl

    names = {}
    pending = {}

    def sem(name):
        return sems.at[names.setdefault(name, len(names))]

    def col(z_, xl_, k_):
        return z_ * 4 + xl_ * 2 + k_

    def remote(src, dst, send_sem, recv_sem, row_, col_):
        return pltpu.make_async_remote_copy(
            src_ref=src, dst_ref=dst, send_sem=send_sem, recv_sem=recv_sem, device_id=(row_, col_), device_id_type=MESH
        )

    def expect(name, ref):
        pending[name] = lambda: pltpu.make_async_copy(ref, ref, sem(name)).wait()

    def need(*keys):
        for key in keys:
            pending.pop(key)()

    def send(name, src, dst, row_, col_, arrives):
        copy = remote(src, dst, sem(name + ".send"), sem(name), row_, col_)
        copy.start()
        pending[name + ".send"] = copy.wait_send
        if arrives is not None:
            expect(name, arrives)

    def start_either(src, dst, send_sem, recv_sem, row_, col_):
        mine = jnp.logical_and(row_ == r, col_ == c)

        @pl.when(mine)
        def _():
            pltpu.make_async_copy(src, dst, recv_sem).start()

        @pl.when(jnp.logical_not(mine))
        def _():
            remote(src, dst, send_sem, recv_sem, row_, col_).start()

    def body():
        pat_copy = pltpu.make_async_copy(pat_hbm, pat, sem("pat"))
        pat_copy.start()
        pending["pat"] = pat_copy.wait

        barrier = pltpu.get_barrier_semaphore()

        def greet(row_, col_):
            pl.semaphore_signal(barrier, inc=1, device_id=(row_, col_), device_id_type=MESH)

        def greet_col(j, carry):
            greet(r, (c + j) % 32)
            return carry

        lax.fori_loop(1, 32, greet_col, 0)

        def greet_row(j, carry):
            greet((r + j) % 8, c)
            greet((r + j) % 8, col(z, xl, 1 - k))
            return carry

        lax.fori_loop(1, 8, greet_row, 0)
        greet(2 * y + 1 - xh, col(z, 1 - xl, k))
        pd_src_row = 2 * ((z % 2) * 2 + xl) + (z % 4) // 2
        for x_src in range(2):
            src_col = col(r, x_src, k)

            @pl.when(jnp.logical_not(jnp.logical_and(pd_src_row == r, src_col == c)))
            def _():
                greet(pd_src_row, src_col)

        others = 31 + 14 + 1
        pd_mine = []
        for t in range(2):
            mine = jnp.logical_and(z == r, col(4 * t + 2 * xh + y // 2, y % 2, k) == c)
            pd_mine.append(mine)
            others = others + jnp.where(mine, jnp.int32(0), jnp.int32(1))
        pl.semaphore_wait(barrier, others)
        if STOP == "greet":
            return

        def send_a(j, carry):
            zi, xi, s = 4 * k + j // 4, (j // 2) % 2, j % 2
            src = pan.at[
                s, pl.ds(pl.multiple_of(32 * y + 8 * (j // 4), 8), 8), pl.ds(pl.multiple_of(256 * xi, 256), 256)
            ]
            start_either(src, buf_a.at[q], sem("a.send"), sem("a"), r, col(zi, xi, s))
            return carry

        lax.fori_loop(0, 16, send_a, 0)
        expect("a", buf_a)

        def wait_send_a():
            @pl.when(z // 4 == k)
            def _():
                pltpu.make_async_copy(buf_a.at[pl.ds(0, 15)], buf_a.at[pl.ds(0, 15)], sem("a.send")).wait()

            @pl.when(z // 4 != k)
            def _():
                pltpu.make_async_copy(buf_a, buf_a, sem("a.send")).wait()

        pending["a.send"] = wait_send_a
        if STOP == "a_only":
            return

        own = fbuf.at[y, xh]
        f_own = pltpu.make_async_copy(fin.at[k], own, sem("f_own"))
        f_own.start()
        pending["f_own"] = f_own.wait
        for d in (2, 1, 3):
            send("f%d" % d, fin.at[k], own, 2 * ((y + d) % 4) + xh, c, fbuf.at[(y + 4 - d) % 4, xh])

        quarter = abuf.at[2 * xl + k]
        pltpu.make_async_copy(anc.at[k], quarter, sem("anc")).start()
        for name, s, x_to in (("anc_core", 1 - k, xl), ("anc_x0", 0, 1 - xl), ("anc_x1", 1, 1 - xl)):
            copy = remote(anc.at[s], quarter, sem(name), sem("anc"), r, col(z, x_to, s))
            copy.start()
            pending[name] = copy.wait_send
        expect("anc", abuf)

        need("pat")

        def invert(n, carry):
            found = jnp.int32(0)
            for j in range(16):
                found = jnp.where(pat[k, j] == n, jnp.int32(j), found)
            inv[n] = found
            return carry

        lax.fori_loop(0, 16, invert, 0)
        need("a")
        if STOP == "a":
            return

        b_dst = pbuf.at[:, z // 4, y, pl.ds(pl.multiple_of(8 * (z % 4), 8), 8), :]

        def send_b_to(j, carry):
            zd = (z + j) % 8
            send_b[zd, 0] = buf_a[inv[2 * zd]]
            send_b[zd, 1] = buf_a[inv[2 * zd + 1]]
            remote(send_b.at[zd], b_dst, sem("b.send"), sem("b"), r, col(zd, xl, k)).start()
            return carry

        lax.fori_loop(1, 8, send_b_to, 0)
        send_b[z, 0] = buf_a[inv[2 * z]]
        send_b[z, 1] = buf_a[inv[2 * z + 1]]
        pltpu.make_async_copy(send_b.at[z], b_dst, sem("b")).start()
        expect("b", pbuf.at[:, :, y])
        expect("b.send", send_b.at[pl.ds(0, 7)])
        need("f_own", "f1", "f2", "f3")
        send("f_x", fbuf.at[:, xh], fbuf.at[:, xh], 2 * y + 1 - xh, col(z, 1 - xl, k), fbuf.at[:, 1 - xh])
        if STOP == "f_x1":
            return
        need("b")
        if STOP == "b":
            return

        mine = pbuf.at[:, :, y]
        for d in (2, 1, 3):
            send("c%d" % d, mine, mine, 2 * ((y + d) % 4) + xh, c, pbuf.at[:, :, (y + 4 - d) % 4])
        for t in range(2):
            start_either(
                pbuf.at[t, xh, y], pdiag.at[xl], sem("pd%d.send" % t), sem("pd"),
                z, col(4 * t + 2 * xh + y // 2, y % 2, k),
            )

            def wait_send_pd(t=t):
                @pl.when(jnp.logical_not(pd_mine[t]))
                def _():
                    pltpu.make_async_copy(pdiag.at[0], pdiag.at[0], sem("pd%d.send" % t)).wait()

            pending["pd%d.send" % t] = wait_send_pd
        expect("pd", pdiag)

        need("anc")
        if STOP == "anc":
            return
        for j in range(4):
            high, low = halves(abuf[j])
            a_high[:, 128 * j : 128 * j + 128] = high
            a_low[:, 128 * j : 128 * j + 128] = low

        need("c1", "c2", "c3")
        if STOP == "c2":
            return
        p_high, p_low = halves(pbuf[...].reshape(512, 256))
        cbuf[...] = dot3(a_high[...], a_low[...], p_high, p_low).reshape(16, 32, 256)
        if STOP == "product":
            return

        def send_sum(j, carry):
            zd, xd = (z + (j + 2) // 2) % 8, (xl + j) % 2
            remote(
                cbuf.at[2 * zd + xd], rbuf.at[xl, z], sem("sum.send"), sem("sum"), r, col(zd, xd, k)
            ).start()
            return carry

        lax.fori_loop(0, 14, send_sum, 0)
        remote(cbuf.at[2 * z + 1 - xl], rbuf.at[xl, z], sem("sum.send"), sem("sum"), r, col(z, 1 - xl, k)).start()
        all_but_own = cbuf.at[pl.ds(0, 15)]
        expect("sum", all_but_own)
        expect("sum.send", all_but_own)
        rbuf[xl, z] = cbuf[q]
        need("f_x")
        high, low = halves(fbuf[...].reshape(512, 512))
        f_high[...] = high
        f_low[...] = low
        if STOP == "f_x":
            return
        need("pd")
        s_high, s_low = halves(jnp.concatenate([pdiag[0], pdiag[1]], axis=1))
        spread[...] = dot3(s_high, s_low, f_high[...], f_low[...])
        own_factor = fbuf[y, xh]
        own_sq[...] = jnp.sum(own_factor * own_factor, axis=0, keepdims=True)
        if STOP == "spread":
            return
        need("sum")
        if STOP == "sum":
            return

        y_high, y_low = halves(jnp.concatenate([jnp.sum(rbuf[0], axis=0), jnp.sum(rbuf[1], axis=0)], axis=1))
        result = dot3(y_high, y_low, f_high[...], f_low[...])
        prod[...] = -result.reshape(2, 16, 512)
        send("o", prod.at[1 - k], out_block.at[k], r, col(z, xl, 1 - k), out_block.at[1 - k])
        d_send[...] = jnp.sum(spread[...] * result, axis=0, keepdims=True)
        d1[q] = d_send[...]
        if STOP == "apply":
            return

        def send_d1(j, carry):
            remote(d_send, d1.at[q], sem("d1.send"), sem("d1"), r, (c + 2 * j) % 32).start()
            return carry

        lax.fori_loop(1, 16, send_d1, 0)
        some = d1.at[pl.ds(0, 15)]
        expect("d1", some)
        expect("d1.send", some)
        out_block[k] = prod[k]
        need("d1")
        if STOP == "d1":
            return
        d1_sum[...] = jnp.sum(d1[...], axis=0) + own_sq[...]
        d2[k, r] = d1_sum[...]

        def send_d2(j, carry):
            remote(d1_sum, d2.at[k, r], sem("d2.send"), sem("d2"), (r + j) % 8, c).start()
            remote(d1_sum, d2.at[k, r], sem("d2.send"), sem("d2"), (r + j) % 8, col(z, xl, 1 - k)).start()
            return carry

        lax.fori_loop(1, 8, send_d2, 0)
        remote(d1_sum, d2.at[k, r], sem("d2.send"), sem("d2"), r, col(z, xl, 1 - k)).start()
        expect("d2", some)
        expect("d2.send", some)
        need("d2")
        for s in range(2):
            out_diag[pl.ds(s, 1), :] = jnp.sum(d2[s], axis=0)

    body()
    need(*pending)


def per_device(ancestor, panel, factor_inv, pattern):
    vmem = pltpu.VMEM
    return pl.pallas_call(
        kernel,
        out_shape=(jax.ShapeDtypeStruct((2, 16, 512), F32), jax.ShapeDtypeStruct((2, 512), F32)),
        in_specs=[pl.BlockSpec(memory_space=pl.ANY)] * 4,
        out_specs=(pl.BlockSpec(memory_space=vmem), pl.BlockSpec(memory_space=vmem)),
        scratch_shapes=[
            pltpu.SMEM((2, 16), jnp.int32),
            pltpu.SMEM((16,), jnp.int32),
            vmem((16, 8, 256), F32),
            vmem((8, 2, 8, 256), F32),
            vmem((2, 2, 4, 32, 256), F32),
            vmem((4, 512, 128), F32),
            vmem((4, 2, 64, 512), F32),
            vmem((16, 32, 256), F32),
            vmem((2, 8, 32, 256), F32),
            vmem((2, 32, 256), F32),
            vmem((32, 512), F32),
            vmem((2, 16, 512), F32),
            vmem((1, 512), F32),
            vmem((1, 512), F32),
            vmem((16, 1, 512), F32),
            vmem((1, 512), F32),
            vmem((2, 8, 1, 512), F32),
            vmem((512, 512), BF16),
            vmem((512, 512), BF16),
            vmem((512, 512), BF16),
            vmem((512, 512), BF16),
            pltpu.SemaphoreType.DMA((80,)),
        ],
        compiler_params=pltpu.CompilerParams(
            collective_id=0, has_side_effects=True, vmem_limit_bytes=60 * 1024 * 1024
        ),
    )(ancestor, panel, factor_inv, pattern)


def solution(mesh):
    in_specs = (P(None, "row", "col"), P(None, "col", None), P(None, "row", None), P())
    out_specs = (P(None, ("row", "col"), None), P())
    return jax.shard_map(per_device, mesh=mesh, in_specs=in_specs, out_specs=out_specs, check_vma=False)
```

```python
import jax
import jax.numpy as jnp
from jax import lax
from jax.experimental import pallas as pl
from jax.experimental.pallas import tpu as pltpu
from jax.sharding import PartitionSpec as P


MESH = pl.DeviceIdType.MESH
F32 = jnp.float32
BF16 = jnp.bfloat16


def halves(x):
    high = x.astype(BF16)
    low = (x - high.astype(F32)).astype(BF16)
    return high, low


def dot3(a_high, a_low, b_high, b_low):
    def dot(a, b):
        return jnp.dot(a, b, preferred_element_type=F32)

    return dot(a_high, b_high) + (dot(a_low, b_high) + dot(a_high, b_low))


def times_factor(x, f_high, f_low):
    high, low = halves(x)
    both = jnp.concatenate([high, low], axis=0)
    n = x.shape[0]

    def part(first, cols):
        rows = slice(first, 512)
        twice = jnp.dot(both[:, rows], f_high[rows, cols], preferred_element_type=F32)
        return twice[:n] + (twice[n:] + jnp.dot(high[:, rows], f_low[rows, cols], preferred_element_type=F32))

    return jnp.concatenate([part(0, slice(0, 256)), part(256, slice(256, 512))], axis=1)


def kernel(
    anc, pan, fin, pat_hbm, out_block, out_diag,
    pat, inv, buf_a, send_b, pbuf, abuf, fbuf, cbuf, rbuf, pdiag, spread, prod, d_send, own_sq, d1, d1_sum, d2,
    a_high, a_low, f_high, f_low, sems, b_sems,
):
    r = lax.axis_index("row")
    c = lax.axis_index("col")
    y, xh = r // 2, r % 2
    z, xl, k = c // 4, (c // 2) % 2, c % 2
    q = 2 * z + xl

    names = {}
    pending = {}

    def sem(name):
        return sems.at[names.setdefault(name, len(names))]

    def col(z_, xl_, k_):
        return z_ * 4 + xl_ * 2 + k_

    def remote(src, dst, send_sem, recv_sem, row_, col_):
        return pltpu.make_async_remote_copy(
            src_ref=src, dst_ref=dst, send_sem=send_sem, recv_sem=recv_sem, device_id=(row_, col_), device_id_type=MESH
        )

    def expect(name, ref):
        pending[name] = lambda: pltpu.make_async_copy(ref, ref, sem(name)).wait()

    def need(*keys):
        for key in keys:
            pending.pop(key)()

    def send(name, src, dst, row_, col_, arrives):
        copy = remote(src, dst, sem(name + ".send"), sem(name), row_, col_)
        copy.start()
        pending[name + ".send"] = copy.wait_send
        if arrives is not None:
            expect(name, arrives)

    def start_either(src, dst, send_sem, recv_sem, row_, col_):
        mine = jnp.logical_and(row_ == r, col_ == c)

        @pl.when(mine)
        def _():
            pltpu.make_async_copy(src, dst, recv_sem).start()

        @pl.when(jnp.logical_not(mine))
        def _():
            remote(src, dst, send_sem, recv_sem, row_, col_).start()

    def far_first(j):
        half = (j + 1) // 2
        return 4 + jnp.where(j % 2 == 1, -half, half)

    def near_first(j):
        half = j // 2 + 1
        return jnp.where(j % 2 == 0, half, 8 - half)

    def body():
        pat_copy = pltpu.make_async_copy(pat_hbm, pat, sem("pat"))
        pat_copy.start()
        pending["pat"] = pat_copy.wait

        barrier = pltpu.get_barrier_semaphore()

        def greet(row_, col_):
            pl.semaphore_signal(barrier, inc=1, device_id=(row_, col_), device_id_type=MESH)

        def greet_col(j, carry):
            greet(r, (c + j) % 32)
            return carry

        lax.fori_loop(1, 32, greet_col, 0)

        def greet_row(j, carry):
            greet((r + j) % 8, c)
            greet((r + j) % 8, col(z, xl, 1 - k))
            return carry

        lax.fori_loop(1, 8, greet_row, 0)
        greet(2 * y + 1 - xh, col(z, 1 - xl, k))
        pd_src_row = 2 * ((z % 2) * 2 + xl) + (z % 4) // 2
        for x_src in range(2):
            src_col = col(r, x_src, k)

            @pl.when(jnp.logical_not(jnp.logical_and(pd_src_row == r, src_col == c)))
            def _():
                greet(pd_src_row, src_col)

        others = 31 + 14 + 1
        pd_mine = []
        for t in range(2):
            mine = jnp.logical_and(z == r, col(4 * t + 2 * xh + y // 2, y % 2, k) == c)
            pd_mine.append(mine)
            others = others + jnp.where(mine, jnp.int32(0), jnp.int32(1))
        pl.semaphore_wait(barrier, others)

        def piece(zi, xi, s):
            return pan.at[
                s, pl.ds(pl.multiple_of(32 * y + 8 * (zi % 4), 8), 8), pl.ds(pl.multiple_of(256 * xi, 256), 256)
            ]

        def send_a(j, carry):
            zi, xi, s = 4 * k + (z + j // 4) % 4, (xl + j // 2) % 2, (k + j) % 2
            remote(piece(zi, xi, s), buf_a.at[q], sem("a.send"), sem("a"), r, col(zi, xi, s)).start()
            return carry

        lax.fori_loop(1, 16, send_a, 0)
        first = 4 * k + z % 4
        start_either(piece(first, xl, k), buf_a.at[q], sem("a.send"), sem("a"), r, col(first, xl, k))
        expect("a", buf_a)

        def wait_send_a():
            @pl.when(z // 4 == k)
            def _():
                pltpu.make_async_copy(buf_a.at[pl.ds(0, 15)], buf_a.at[pl.ds(0, 15)], sem("a.send")).wait()

            @pl.when(z // 4 != k)
            def _():
                pltpu.make_async_copy(buf_a, buf_a, sem("a.send")).wait()

        pending["a.send"] = wait_send_a

        own = fbuf.at[y, xh]
        f_own = pltpu.make_async_copy(fin.at[k], own, sem("f_own"))
        f_own.start()
        pending["f_own"] = f_own.wait
        for d in (2, 1, 3):
            send("f%d" % d, fin.at[k], own, 2 * ((y + d) % 4) + xh, c, fbuf.at[(y + 4 - d) % 4, xh])

        quarter = abuf.at[2 * xl + k]
        pltpu.make_async_copy(anc.at[k], quarter, sem("anc")).start()
        for name, s, x_to in (("anc_core", 1 - k, xl), ("anc_x0", 0, 1 - xl), ("anc_x1", 1, 1 - xl)):
            copy = remote(anc.at[s], quarter, sem(name), sem("anc"), r, col(z, x_to, s))
            copy.start()
            pending[name] = copy.wait_send
        expect("anc", abuf)

        need("pat")

        def invert(n, carry):
            found = jnp.int32(0)
            for j in range(16):
                found = jnp.where(pat[k, j] == n, jnp.int32(j), found)
            inv[n] = found
            return carry

        lax.fori_loop(0, 16, invert, 0)
        need("a")

        def b_place(zi):
            return pbuf.at[:, zi // 4, y, pl.ds(pl.multiple_of(8 * (zi % 4), 8), 8), :]

        def choose(zd):
            send_b[zd, 0] = buf_a[inv[2 * zd]]
            send_b[zd, 1] = buf_a[inv[2 * zd + 1]]

        def send_b_to(j, carry):
            d = near_first(j)
            zd = (z + d) % 8
            choose(zd)
            remote(send_b.at[zd], b_place(z), sem("b.send"), b_sems.at[d], r, col(zd, xl, k)).start()
            return carry

        choose(z)
        pltpu.make_async_copy(send_b.at[z], b_place(z), b_sems.at[0]).start()
        lax.fori_loop(0, 7, send_b_to, 0)
        expect("b.send", send_b.at[pl.ds(0, 7)])

        need("f_own", "f1", "f2", "f3")
        send("f_x", fbuf.at[:, xh], fbuf.at[:, xh], 2 * y + 1 - xh, col(z, 1 - xl, k), fbuf.at[:, 1 - xh])

        for d in (0, 1, 7, 2, 6, 3, 5, 4):
            place = b_place((z + 8 - d) % 8)
            pltpu.make_async_copy(place, place, b_sems.at[d]).wait()
            for dy in (2, 1, 3):
                remote(place, place, sem("c.send"), sem("c"), 2 * ((y + dy) % 4) + xh, c).start()
        three = pbuf.at[:, :, pl.ds(0, 3)]
        expect("c", three)
        expect("c.send", three)
        for t in range(2):
            start_either(
                pbuf.at[t, xh, y], pdiag.at[xl], sem("pd%d.send" % t), sem("pd"),
                z, col(4 * t + 2 * xh + y // 2, y % 2, k),
            )

            def wait_send_pd(t=t):
                @pl.when(jnp.logical_not(pd_mine[t]))
                def _():
                    pltpu.make_async_copy(pdiag.at[0], pdiag.at[0], sem("pd%d.send" % t)).wait()

            pending["pd%d.send" % t] = wait_send_pd
        expect("pd", pdiag)

        need("anc")
        for j in range(4):
            high, low = halves(abuf[j])
            a_high[:, 128 * j : 128 * j + 128] = high
            a_low[:, 128 * j : 128 * j + 128] = low

        need("c")
        p_high, p_low = halves(pbuf[...].reshape(512, 256))
        cbuf[...] = dot3(a_high[...], a_low[...], p_high, p_low).reshape(16, 32, 256)

        def send_sum(j, carry):
            zd, xd = (z + far_first(j // 2)) % 8, (xl + 1 + j) % 2
            remote(
                cbuf.at[2 * zd + xd], rbuf.at[xl, z], sem("sum.send"), sem("sum"), r, col(zd, xd, k)
            ).start()
            return carry

        lax.fori_loop(0, 14, send_sum, 0)
        remote(cbuf.at[2 * z + 1 - xl], rbuf.at[xl, z], sem("sum.send"), sem("sum"), r, col(z, 1 - xl, k)).start()
        all_but_own = cbuf.at[pl.ds(0, 15)]
        expect("sum", all_but_own)
        expect("sum.send", all_but_own)
        rbuf[xl, z] = cbuf[q]
        need("f_x")
        high, low = halves(fbuf[...].reshape(512, 512))
        f_high[...] = high
        f_low[...] = low
        need("pd")
        spread[...] = times_factor(jnp.concatenate([pdiag[0], pdiag[1]], axis=1), f_high, f_low)
        own_factor = fbuf[y, xh]
        own_sq[...] = jnp.sum(own_factor * own_factor, axis=0, keepdims=True)
        need("sum")

        total = jnp.concatenate([jnp.sum(rbuf[0], axis=0), jnp.sum(rbuf[1], axis=0)], axis=1)
        result = times_factor(total, f_high, f_low)
        prod[...] = -result.reshape(2, 16, 512)
        send("o", prod.at[1 - k], out_block.at[k], r, col(z, xl, 1 - k), out_block.at[1 - k])
        d_send[...] = jnp.sum(spread[...] * result, axis=0, keepdims=True)
        d1[q] = d_send[...]

        def send_d1(j, carry):
            remote(d_send, d1.at[q], sem("d1.send"), sem("d1"), r, (c + 2 * j) % 32).start()
            return carry

        lax.fori_loop(1, 16, send_d1, 0)
        some = d1.at[pl.ds(0, 15)]
        expect("d1", some)
        expect("d1.send", some)
        out_block[k] = prod[k]
        need("d1")
        d1_sum[...] = jnp.sum(d1[...], axis=0) + own_sq[...]
        d2[k, r] = d1_sum[...]

        def send_d2(j, carry):
            remote(d1_sum, d2.at[k, r], sem("d2.send"), sem("d2"), (r + j) % 8, c).start()
            remote(d1_sum, d2.at[k, r], sem("d2.send"), sem("d2"), (r + j) % 8, col(z, xl, 1 - k)).start()
            return carry

        lax.fori_loop(1, 8, send_d2, 0)
        remote(d1_sum, d2.at[k, r], sem("d2.send"), sem("d2"), r, col(z, xl, 1 - k)).start()
        expect("d2", some)
        expect("d2.send", some)
        need("d2")
        for s in range(2):
            out_diag[pl.ds(s, 1), :] = jnp.sum(d2[s], axis=0)

    body()
    need(*pending)


def per_device(ancestor, panel, factor_inv, pattern):
    vmem = pltpu.VMEM
    block, diag = pl.pallas_call(
        kernel,
        out_shape=(jax.ShapeDtypeStruct((2, 16, 512), F32), jax.ShapeDtypeStruct((2, 512), F32)),
        in_specs=[pl.BlockSpec(memory_space=pl.ANY)] * 4,
        out_specs=(pl.BlockSpec(memory_space=vmem), pl.BlockSpec(memory_space=vmem)),
        scratch_shapes=[
            pltpu.SMEM((2, 16), jnp.int32),
            pltpu.SMEM((16,), jnp.int32),
            vmem((16, 8, 256), F32),
            vmem((8, 2, 8, 256), F32),
            vmem((2, 2, 4, 32, 256), F32),
            vmem((4, 512, 128), F32),
            vmem((4, 2, 64, 512), F32),
            vmem((16, 32, 256), F32),
            vmem((2, 8, 32, 256), F32),
            vmem((2, 32, 256), F32),
            vmem((32, 512), F32),
            vmem((2, 16, 512), F32),
            vmem((1, 512), F32),
            vmem((1, 512), F32),
            vmem((16, 1, 512), F32),
            vmem((1, 512), F32),
            vmem((2, 8, 1, 512), F32),
            vmem((512, 512), BF16),
            vmem((512, 512), BF16),
            vmem((512, 512), BF16),
            vmem((512, 512), BF16),
            pltpu.SemaphoreType.DMA((48,)),
            pltpu.SemaphoreType.DMA((8,)),
        ],
        compiler_params=pltpu.CompilerParams(
            collective_id=0, has_side_effects=True, vmem_limit_bytes=60 * 1024 * 1024
        ),
    )(ancestor, panel, factor_inv, pattern)
    return block, diag


def solution(mesh):
    in_specs = (P(None, "row", "col"), P(None, "col", None), P(None, "row", None), P())
    out_specs = (P(None, ("row", "col"), None), P())
    return jax.shard_map(per_device, mesh=mesh, in_specs=in_specs, out_specs=out_specs, check_vma=False)
```

```python
import jax
import jax.numpy as jnp
from jax import lax
from jax.experimental import pallas as pl
from jax.experimental.pallas import tpu as pltpu
from jax.sharding import PartitionSpec as P


MESH = pl.DeviceIdType.MESH
F32 = jnp.float32
BF16 = jnp.bfloat16


def halves(x):
    high = x.astype(BF16)
    low = (x - high.astype(F32)).astype(BF16)
    return high, low


def dot3(a_high, a_low, b_high, b_low):
    def dot(a, b):
        return jnp.dot(a, b, preferred_element_type=F32)

    return dot(a_high, b_high) + (dot(a_low, b_high) + dot(a_high, b_low))


def times_factor(x, f_high, f_low):
    high, low = halves(x)
    both = jnp.concatenate([high, low], axis=0)
    n = x.shape[0]

    def part(first, cols):
        rows = slice(first, 512)
        twice = jnp.dot(both[:, rows], f_high[rows, cols], preferred_element_type=F32)
        return twice[:n] + (twice[n:] + jnp.dot(high[:, rows], f_low[rows, cols], preferred_element_type=F32))

    return jnp.concatenate([part(0, slice(0, 256)), part(256, slice(256, 512))], axis=1)


def kernel(
    anc, pan, fin, pat_hbm, out_block, out_diag,
    pat, inv, buf_a, send_b, pbuf, abuf, fbuf, cbuf, rbuf, relay3, relay4, pdiag, spread, prod, d_send, own_sq, d1, d1_sum, d2,
    a_high, a_low, f_high, f_low, sems, b_sems, relay_sems,
):
    r = lax.axis_index("row")
    c = lax.axis_index("col")
    y, xh = r // 2, r % 2
    z, xl, k = c // 4, (c // 2) % 2, c % 2
    q = 2 * z + xl

    names = {}
    pending = {}

    def sem(name):
        return sems.at[names.setdefault(name, len(names))]

    def col(z_, xl_, k_):
        return z_ * 4 + xl_ * 2 + k_

    def remote(src, dst, send_sem, recv_sem, row_, col_):
        return pltpu.make_async_remote_copy(
            src_ref=src, dst_ref=dst, send_sem=send_sem, recv_sem=recv_sem, device_id=(row_, col_), device_id_type=MESH
        )

    def expect(name, ref):
        pending[name] = lambda: pltpu.make_async_copy(ref, ref, sem(name)).wait()

    def need(*keys):
        for key in keys:
            pending.pop(key)()

    def send(name, src, dst, row_, col_, arrives):
        copy = remote(src, dst, sem(name + ".send"), sem(name), row_, col_)
        copy.start()
        pending[name + ".send"] = copy.wait_send
        if arrives is not None:
            expect(name, arrives)

    def start_either(src, dst, send_sem, recv_sem, row_, col_):
        mine = jnp.logical_and(row_ == r, col_ == c)

        @pl.when(mine)
        def _():
            pltpu.make_async_copy(src, dst, recv_sem).start()

        @pl.when(jnp.logical_not(mine))
        def _():
            remote(src, dst, send_sem, recv_sem, row_, col_).start()

    def near_first(j):
        half = j // 2 + 1
        return jnp.where(j % 2 == 0, half, 8 - half)

    def body():
        pat_copy = pltpu.make_async_copy(pat_hbm, pat, sem("pat"))
        pat_copy.start()
        pending["pat"] = pat_copy.wait

        barrier = pltpu.get_barrier_semaphore()

        def greet(row_, col_):
            pl.semaphore_signal(barrier, inc=1, device_id=(row_, col_), device_id_type=MESH)

        def greet_col(j, carry):
            greet(r, (c + j) % 32)
            return carry

        lax.fori_loop(1, 32, greet_col, 0)

        def greet_row(j, carry):
            greet((r + j) % 8, c)
            greet((r + j) % 8, col(z, xl, 1 - k))
            return carry

        lax.fori_loop(1, 8, greet_row, 0)
        greet(2 * y + 1 - xh, col(z, 1 - xl, k))
        pd_src_row = 2 * ((z % 2) * 2 + xl) + (z % 4) // 2
        for x_src in range(2):
            src_col = col(r, x_src, k)

            @pl.when(jnp.logical_not(jnp.logical_and(pd_src_row == r, src_col == c)))
            def _():
                greet(pd_src_row, src_col)

        others = 31 + 14 + 1
        pd_mine = []
        for t in range(2):
            mine = jnp.logical_and(z == r, col(4 * t + 2 * xh + y // 2, y % 2, k) == c)
            pd_mine.append(mine)
            others = others + jnp.where(mine, jnp.int32(0), jnp.int32(1))
        pl.semaphore_wait(barrier, others)

        def piece(zi, xi, s):
            return pan.at[
                s, pl.ds(pl.multiple_of(32 * y + 8 * (zi % 4), 8), 8), pl.ds(pl.multiple_of(256 * xi, 256), 256)
            ]

        def send_a(j, carry):
            zi, xi, s = 4 * k + (z + j // 4) % 4, (xl + j // 2) % 2, (k + j) % 2
            remote(piece(zi, xi, s), buf_a.at[q], sem("a.send"), sem("a"), r, col(zi, xi, s)).start()
            return carry

        lax.fori_loop(1, 16, send_a, 0)
        first = 4 * k + z % 4
        start_either(piece(first, xl, k), buf_a.at[q], sem("a.send"), sem("a"), r, col(first, xl, k))
        expect("a", buf_a)

        def wait_send_a():
            @pl.when(z // 4 == k)
            def _():
                pltpu.make_async_copy(buf_a.at[pl.ds(0, 15)], buf_a.at[pl.ds(0, 15)], sem("a.send")).wait()

            @pl.when(z // 4 != k)
            def _():
                pltpu.make_async_copy(buf_a, buf_a, sem("a.send")).wait()

        pending["a.send"] = wait_send_a

        own = fbuf.at[y, xh]
        f_own = pltpu.make_async_copy(fin.at[k], own, sem("f_own"))
        f_own.start()
        pending["f_own"] = f_own.wait
        for d in (2, 1, 3):
            send("f%d" % d, fin.at[k], own, 2 * ((y + d) % 4) + xh, c, fbuf.at[(y + 4 - d) % 4, xh])

        quarter = abuf.at[2 * xl + k]
        pltpu.make_async_copy(anc.at[k], quarter, sem("anc")).start()
        for name, s, x_to in (("anc_core", 1 - k, xl), ("anc_x0", 0, 1 - xl), ("anc_x1", 1, 1 - xl)):
            copy = remote(anc.at[s], quarter, sem(name), sem("anc"), r, col(z, x_to, s))
            copy.start()
            pending[name] = copy.wait_send
        expect("anc", abuf)

        need("pat")

        def invert(n, carry):
            found = jnp.int32(0)
            for j in range(16):
                found = jnp.where(pat[k, j] == n, jnp.int32(j), found)
            inv[n] = found
            return carry

        lax.fori_loop(0, 16, invert, 0)
        need("a")

        def b_place(zi):
            return pbuf.at[:, zi // 4, y, pl.ds(pl.multiple_of(8 * (zi % 4), 8), 8), :]

        def choose(zd):
            send_b[zd, 0] = buf_a[inv[2 * zd]]
            send_b[zd, 1] = buf_a[inv[2 * zd + 1]]

        def send_b_to(j, carry):
            d = near_first(j)
            zd = (z + d) % 8
            choose(zd)
            remote(send_b.at[zd], b_place(z), sem("b.send"), b_sems.at[d], r, col(zd, xl, k)).start()
            return carry

        choose(z)
        pltpu.make_async_copy(send_b.at[z], b_place(z), b_sems.at[0]).start()
        lax.fori_loop(0, 7, send_b_to, 0)
        expect("b.send", send_b.at[pl.ds(0, 7)])

        need("f_own", "f1", "f2", "f3")
        send("f_x", fbuf.at[:, xh], fbuf.at[:, xh], 2 * y + 1 - xh, col(z, 1 - xl, k), fbuf.at[:, 1 - xh])

        for d in (0, 1, 7, 2, 6, 3, 5, 4):
            place = b_place((z + 8 - d) % 8)
            pltpu.make_async_copy(place, place, b_sems.at[d]).wait()
            for dy in (2, 1, 3):
                remote(place, place, sem("c.send"), sem("c"), 2 * ((y + dy) % 4) + xh, c).start()
        three = pbuf.at[:, :, pl.ds(0, 3)]
        expect("c", three)
        expect("c.send", three)
        for t in range(2):
            start_either(
                pbuf.at[t, xh, y], pdiag.at[xl], sem("pd%d.send" % t), sem("pd"),
                z, col(4 * t + 2 * xh + y // 2, y % 2, k),
            )

            def wait_send_pd(t=t):
                @pl.when(jnp.logical_not(pd_mine[t]))
                def _():
                    pltpu.make_async_copy(pdiag.at[0], pdiag.at[0], sem("pd%d.send" % t)).wait()

            pending["pd%d.send" % t] = wait_send_pd
        expect("pd", pdiag)

        need("anc")
        for j in range(4):
            high, low = halves(abuf[j])
            a_high[:, 128 * j : 128 * j + 128] = high
            a_low[:, 128 * j : 128 * j + 128] = low

        need("c")
        p_high, p_low = halves(pbuf[...].reshape(512, 256))
        cbuf[...] = dot3(a_high[...], a_low[...], p_high, p_low).reshape(16, 32, 256)

        ways = ((1, pl.ds(0, 128)), (7, pl.ds(128, 128)))
        xs = ((xl + 1) % 2, xl)
        for i, xd in enumerate(xs):
            for w, (up, half) in enumerate(ways):
                remote(
                    cbuf.at[2 * ((z + 4) % 8) + xd, :, half], relay4.at[w, i],
                    sem("relay.send"), relay_sems.at[w, i, 0], r, col((z + 2 * up) % 8, xl, k),
                ).start()
                remote(
                    cbuf.at[2 * ((z + 3 * up) % 8) + xd], relay3.at[w, i],
                    sem("relay.send"), relay_sems.at[w, i, 1], r, col((z + up) % 8, xl, k),
                ).start()

        def send_sum(zd, xd, slot):
            remote(cbuf.at[2 * zd + xd], rbuf.at[xl, slot], sem("sum.send"), sem("sum"), r, col(zd, xd, k)).start()

        for xd in xs:
            for w, (up, half) in enumerate(ways):
                send_sum((z + up) % 8, xd, 1 + w)
        send_sum(z, 1 - xl, 0)
        rbuf[xl, 0] = cbuf[q]
        expect("relay.send", cbuf.at[pl.ds(0, 6)])
        expect("sum", cbuf.at[pl.ds(0, 9)])
        expect("sum.send", cbuf.at[pl.ds(0, 9)])
        for i, xd in enumerate(xs):
            for w, (up, half) in enumerate(ways):
                pltpu.make_async_copy(relay4.at[w, i], relay4.at[w, i], relay_sems.at[w, i, 0]).wait()
                pltpu.make_async_copy(relay3.at[w, i], relay3.at[w, i], relay_sems.at[w, i, 1]).wait()
                zd = (z + 2 * up) % 8
                cbuf[2 * zd + xd] += relay3[w, i]
                cbuf[2 * zd + xd, :, half] += relay4[w, i]
                send_sum(zd, xd, 3 + w)
        need("f_x")
        high, low = halves(fbuf[...].reshape(512, 512))
        f_high[...] = high
        f_low[...] = low
        need("pd")
        spread[...] = times_factor(jnp.concatenate([pdiag[0], pdiag[1]], axis=1), f_high, f_low)
        own_factor = fbuf[y, xh]
        own_sq[...] = jnp.sum(own_factor * own_factor, axis=0, keepdims=True)
        need("sum")

        total = jnp.concatenate([jnp.sum(rbuf[0], axis=0), jnp.sum(rbuf[1], axis=0)], axis=1)
        result = times_factor(total, f_high, f_low)
        prod[...] = -result.reshape(2, 16, 512)
        send("o", prod.at[1 - k], out_block.at[k], r, col(z, xl, 1 - k), out_block.at[1 - k])
        d_send[...] = jnp.sum(spread[...] * result, axis=0, keepdims=True)
        d1[q] = d_send[...]

        def send_d1(j, carry):
            remote(d_send, d1.at[q], sem("d1.send"), sem("d1"), r, (c + 2 * j) % 32).start()
            return carry

        lax.fori_loop(1, 16, send_d1, 0)
        some = d1.at[pl.ds(0, 15)]
        expect("d1", some)
        expect("d1.send", some)
        out_block[k] = prod[k]
        need("d1")
        d1_sum[...] = jnp.sum(d1[...], axis=0) + own_sq[...]
        d2[k, r] = d1_sum[...]

        def send_d2(j, carry):
            remote(d1_sum, d2.at[k, r], sem("d2.send"), sem("d2"), (r + j) % 8, c).start()
            remote(d1_sum, d2.at[k, r], sem("d2.send"), sem("d2"), (r + j) % 8, col(z, xl, 1 - k)).start()
            return carry

        lax.fori_loop(1, 8, send_d2, 0)
        remote(d1_sum, d2.at[k, r], sem("d2.send"), sem("d2"), r, col(z, xl, 1 - k)).start()
        expect("d2", some)
        expect("d2.send", some)
        need("d2")
        for s in range(2):
            out_diag[pl.ds(s, 1), :] = jnp.sum(d2[s], axis=0)

    body()
    need(*pending)


def per_device(ancestor, panel, factor_inv, pattern):
    vmem = pltpu.VMEM
    block, diag = pl.pallas_call(
        kernel,
        out_shape=(jax.ShapeDtypeStruct((2, 16, 512), F32), jax.ShapeDtypeStruct((2, 512), F32)),
        in_specs=[pl.BlockSpec(memory_space=pl.ANY)] * 4,
        out_specs=(pl.BlockSpec(memory_space=vmem), pl.BlockSpec(memory_space=vmem)),
        scratch_shapes=[
            pltpu.SMEM((2, 16), jnp.int32),
            pltpu.SMEM((16,), jnp.int32),
            vmem((16, 8, 256), F32),
            vmem((8, 2, 8, 256), F32),
            vmem((2, 2, 4, 32, 256), F32),
            vmem((4, 512, 128), F32),
            vmem((4, 2, 64, 512), F32),
            vmem((16, 32, 256), F32),
            vmem((2, 5, 32, 256), F32),
            vmem((2, 2, 32, 256), F32),
            vmem((2, 2, 32, 128), F32),
            vmem((2, 32, 256), F32),
            vmem((32, 512), F32),
            vmem((2, 16, 512), F32),
            vmem((1, 512), F32),
            vmem((1, 512), F32),
            vmem((16, 1, 512), F32),
            vmem((1, 512), F32),
            vmem((2, 8, 1, 512), F32),
            vmem((512, 512), BF16),
            vmem((512, 512), BF16),
            vmem((512, 512), BF16),
            vmem((512, 512), BF16),
            pltpu.SemaphoreType.DMA((48,)),
            pltpu.SemaphoreType.DMA((8,)),
            pltpu.SemaphoreType.DMA((2, 2, 2)),
        ],
        compiler_params=pltpu.CompilerParams(
            collective_id=0, has_side_effects=True, vmem_limit_bytes=32 * 1024 * 1024
        ),
    )(*[pltpu.with_memory_space_constraint(x, pltpu.HBM) for x in (ancestor, panel, factor_inv, pattern)])
    return block, diag


def solution(mesh):
    in_specs = (P(None, "row", "col"), P(None, "col", None), P(None, "row", None), P())
    out_specs = (P(None, ("row", "col"), None), P())
    return jax.shard_map(per_device, mesh=mesh, in_specs=in_specs, out_specs=out_specs, check_vma=False)
```

```python
import jax
import jax.numpy as jnp
from jax import lax
from jax.experimental import pallas as pl
from jax.experimental.pallas import tpu as pltpu
from jax.sharding import PartitionSpec as P


MESH = pl.DeviceIdType.MESH
F32 = jnp.float32
BF16 = jnp.bfloat16


def halves(x):
    high = x.astype(BF16)
    low = (x - high.astype(F32)).astype(BF16)
    return high, low


def dot3(a_high, a_low, b_high, b_low):
    def dot(a, b):
        return jnp.dot(a, b, preferred_element_type=F32)

    return dot(a_high, b_high) + (dot(a_low, b_high) + dot(a_high, b_low))


def times_factor(x, f_high, f_low):
    high, low = halves(x)
    both = jnp.concatenate([high, low], axis=0)
    n = x.shape[0]

    def part(first, cols):
        rows = slice(first, 512)
        twice = jnp.dot(both[:, rows], f_high[rows, cols], preferred_element_type=F32)
        return twice[:n] + (twice[n:] + jnp.dot(high[:, rows], f_low[rows, cols], preferred_element_type=F32))

    return jnp.concatenate([part(0, slice(0, 256)), part(256, slice(256, 512))], axis=1)


def kernel(
    anc, pan, fin, pat_hbm, out_block, out_diag,
    pat, inv, buf_a, send_b, pbuf, abuf, fbuf, send_p, cbuf, rbuf, relay3, relay4, pdiag, spread, prod, d_send, own_sq, d1, d1_sum, d2,
    a_high, a_low, f_high, f_low, sems, b_sems, relay_sems,
):
    r = lax.axis_index("row")
    c = lax.axis_index("col")
    y, xh = r // 2, r % 2
    z, xl, k = c // 4, (c // 2) % 2, c % 2
    q = 2 * z + xl

    names = {}
    pending = {}

    def sem(name):
        return sems.at[names.setdefault(name, len(names))]

    def col(z_, xl_, k_):
        return z_ * 4 + xl_ * 2 + k_

    def remote(src, dst, send_sem, recv_sem, row_, col_):
        return pltpu.make_async_remote_copy(
            src_ref=src, dst_ref=dst, send_sem=send_sem, recv_sem=recv_sem, device_id=(row_, col_), device_id_type=MESH
        )

    def expect(name, ref):
        pending[name] = lambda: pltpu.make_async_copy(ref, ref, sem(name)).wait()

    def need(*keys):
        for key in keys:
            pending.pop(key)()

    def send(name, src, dst, row_, col_, arrives):
        copy = remote(src, dst, sem(name + ".send"), sem(name), row_, col_)
        copy.start()
        pending[name + ".send"] = copy.wait_send
        if arrives is not None:
            expect(name, arrives)

    def start_either(src, dst, send_sem, recv_sem, row_, col_):
        mine = jnp.logical_and(row_ == r, col_ == c)

        @pl.when(mine)
        def _():
            pltpu.make_async_copy(src, dst, recv_sem).start()

        @pl.when(jnp.logical_not(mine))
        def _():
            remote(src, dst, send_sem, recv_sem, row_, col_).start()

    def near_first(j):
        half = j // 2 + 1
        return jnp.where(j % 2 == 0, half, 8 - half)

    def body():
        pat_copy = pltpu.make_async_copy(pat_hbm, pat, sem("pat"))
        pat_copy.start()
        pending["pat"] = pat_copy.wait

        barrier = pltpu.get_barrier_semaphore()

        def greet(row_, col_):
            pl.semaphore_signal(barrier, inc=1, device_id=(row_, col_), device_id_type=MESH)

        def greet_col(j, carry):
            greet(r, (c + j) % 32)
            return carry

        lax.fori_loop(1, 32, greet_col, 0)

        def greet_row(j, carry):
            greet((r + j) % 8, c)
            greet((r + j) % 8, col(z, xl, 1 - k))
            return carry

        lax.fori_loop(1, 8, greet_row, 0)
        greet(2 * y + 1 - xh, col(z, 1 - xl, k))
        pl.semaphore_wait(barrier, 31 + 14 + 1)

        pd_to, pd_x = 2 * (z // 4) + y // 2, y % 2
        pd_self = jnp.logical_and(z % 4 == pd_to, xl == pd_x)

        def piece(zi, xi, s):
            return pan.at[
                s, pl.ds(pl.multiple_of(32 * y + 8 * (zi % 4), 8), 8), pl.ds(pl.multiple_of(256 * xi, 256), 256)
            ]

        def send_a(j, carry):
            zi, xi, s = 4 * k + (z + j // 4) % 4, (xl + j // 2) % 2, (k + j) % 2
            remote(piece(zi, xi, s), buf_a.at[q], sem("a.send"), sem("a"), r, col(zi, xi, s)).start()
            return carry

        lax.fori_loop(1, 16, send_a, 0)
        first = 4 * k + z % 4
        start_either(piece(first, xl, k), buf_a.at[q], sem("a.send"), sem("a"), r, col(first, xl, k))
        expect("a", buf_a)

        def wait_send_a():
            @pl.when(z // 4 == k)
            def _():
                pltpu.make_async_copy(buf_a.at[pl.ds(0, 15)], buf_a.at[pl.ds(0, 15)], sem("a.send")).wait()

            @pl.when(z // 4 != k)
            def _():
                pltpu.make_async_copy(buf_a, buf_a, sem("a.send")).wait()

        pending["a.send"] = wait_send_a

        own = fbuf.at[y, xh]
        f_own = pltpu.make_async_copy(fin.at[k], own, sem("f_own"))
        f_own.start()
        pending["f_own"] = f_own.wait
        for d in (2, 1, 3):
            send("f%d" % d, fin.at[k], own, 2 * ((y + d) % 4) + xh, c, fbuf.at[(y + 4 - d) % 4, xh])

        quarter = abuf.at[2 * xl + k]
        pltpu.make_async_copy(anc.at[k], quarter, sem("anc")).start()
        for name, s, x_to in (("anc_core", 1 - k, xl), ("anc_x0", 0, 1 - xl), ("anc_x1", 1, 1 - xl)):
            copy = remote(anc.at[s], quarter, sem(name), sem("anc"), r, col(z, x_to, s))
            copy.start()
            pending[name] = copy.wait_send
        expect("anc", abuf)

        need("pat")

        def invert(n, carry):
            found = jnp.int32(0)
            for j in range(16):
                found = jnp.where(pat[k, j] == n, jnp.int32(j), found)
            inv[n] = found
            return carry

        lax.fori_loop(0, 16, invert, 0)
        need("a")

        def b_place(zi):
            return pbuf.at[:, zi // 4, y, pl.ds(pl.multiple_of(8 * (zi % 4), 8), 8), :]

        def choose(zd):
            send_b[zd, 0] = buf_a[inv[2 * zd]]
            send_b[zd, 1] = buf_a[inv[2 * zd + 1]]

        def send_b_to(j, carry):
            d = near_first(j)
            zd = (z + d) % 8
            choose(zd)
            remote(send_b.at[zd], b_place(z), sem("b.send"), b_sems.at[d], r, col(zd, xl, k)).start()
            return carry

        choose(z)
        pltpu.make_async_copy(send_b.at[z], b_place(z), b_sems.at[0]).start()
        lax.fori_loop(0, 7, send_b_to, 0)
        expect("b.send", send_b.at[pl.ds(0, 7)])

        need("f_own", "f1", "f2", "f3")
        send("f_x", fbuf.at[:, xh], fbuf.at[:, xh], 2 * y + 1 - xh, col(z, 1 - xl, k), fbuf.at[:, 1 - xh])

        def send_pd(j, carry):
            yd, t = (y + j // 2) % 4, j % 2
            send_p[j] = buf_a[inv[2 * (2 * yd + xh) + t]]
            place = pdiag.at[xl, pl.ds(pl.multiple_of(8 * (z % 4), 8), 8), :]
            to_row, to_col = 2 * yd + xh, col(pd_to + 4 * t, pd_x, k)

            def away():
                remote(send_p.at[j], place, sem("pd.send"), sem("pd"), to_row, to_col).start()

            if isinstance(j, int):
                mine = to_col == c
                pl.when(mine)(lambda: pltpu.make_async_copy(send_p.at[j], place, sem("pd")).start())
                pl.when(jnp.logical_not(mine))(away)
            else:
                away()
            return carry

        lax.fori_loop(2, 8, send_pd, 0)
        send_pd(0, 0)
        send_pd(1, 0)
        expect("pd", pdiag)

        def wait_send_pd():
            def wait_some(n):
                some = send_p.at[pl.ds(0, n)]
                pltpu.make_async_copy(some, some, sem("pd.send")).wait()

            pl.when(pd_self)(lambda: wait_some(7))
            pl.when(jnp.logical_not(pd_self))(lambda: wait_some(8))

        pending["pd.send"] = wait_send_pd

        for d in (0, 1, 7, 2, 6, 3, 5, 4):
            place = b_place((z + 8 - d) % 8)
            pltpu.make_async_copy(place, place, b_sems.at[d]).wait()
            for dy in (2, 1, 3):
                remote(place, place, sem("c.send"), sem("c"), 2 * ((y + dy) % 4) + xh, c).start()
        three = pbuf.at[:, :, pl.ds(0, 3)]
        expect("c", three)
        expect("c.send", three)

        need("anc")
        for j in range(4):
            high, low = halves(abuf[j])
            a_high[:, 128 * j : 128 * j + 128] = high
            a_low[:, 128 * j : 128 * j + 128] = low

        need("c")
        p_high, p_low = halves(pbuf[...].reshape(512, 256))
        cbuf[...] = dot3(a_high[...], a_low[...], p_high, p_low).reshape(16, 32, 256)

        ways = ((1, pl.ds(0, 128)), (7, pl.ds(128, 128)))
        xs = ((xl + 1) % 2, xl)
        for i, xd in enumerate(xs):
            for w, (up, half) in enumerate(ways):
                remote(
                    cbuf.at[2 * ((z + 4) % 8) + xd, :, half], relay4.at[w, i],
                    sem("relay.send"), relay_sems.at[w, i, 0], r, col((z + 2 * up) % 8, xl, k),
                ).start()
                remote(
                    cbuf.at[2 * ((z + 3 * up) % 8) + xd], relay3.at[w, i],
                    sem("relay.send"), relay_sems.at[w, i, 1], r, col((z + up) % 8, xl, k),
                ).start()

        def send_sum(zd, xd, slot):
            remote(cbuf.at[2 * zd + xd], rbuf.at[xl, slot], sem("sum.send"), sem("sum"), r, col(zd, xd, k)).start()

        for xd in xs:
            for w, (up, half) in enumerate(ways):
                send_sum((z + up) % 8, xd, 1 + w)
        send_sum(z, 1 - xl, 0)
        rbuf[xl, 0] = cbuf[q]
        expect("relay.send", cbuf.at[pl.ds(0, 6)])
        expect("sum", cbuf.at[pl.ds(0, 9)])
        expect("sum.send", cbuf.at[pl.ds(0, 9)])
        for i, xd in enumerate(xs):
            for w, (up, half) in enumerate(ways):
                pltpu.make_async_copy(relay4.at[w, i], relay4.at[w, i], relay_sems.at[w, i, 0]).wait()
                pltpu.make_async_copy(relay3.at[w, i], relay3.at[w, i], relay_sems.at[w, i, 1]).wait()
                zd = (z + 2 * up) % 8
                cbuf[2 * zd + xd] += relay3[w, i]
                cbuf[2 * zd + xd, :, half] += relay4[w, i]
                send_sum(zd, xd, 3 + w)
        need("f_x")
        high, low = halves(fbuf[...].reshape(512, 512))
        f_high[...] = high
        f_low[...] = low
        need("pd")
        spread[...] = times_factor(jnp.concatenate([pdiag[0], pdiag[1]], axis=1), f_high, f_low)
        own_factor = fbuf[y, xh]
        own_sq[...] = jnp.sum(own_factor * own_factor, axis=0, keepdims=True)
        need("sum")

        total = jnp.concatenate([jnp.sum(rbuf[0], axis=0), jnp.sum(rbuf[1], axis=0)], axis=1)
        result = times_factor(total, f_high, f_low)
        prod[...] = -result.reshape(2, 16, 512)
        send("o", prod.at[1 - k], out_block.at[k], r, col(z, xl, 1 - k), out_block.at[1 - k])
        d_send[...] = jnp.sum(spread[...] * result, axis=0, keepdims=True)
        d1[q] = d_send[...]

        def send_d1(j, carry):
            remote(d_send, d1.at[q], sem("d1.send"), sem("d1"), r, (c + 2 * j) % 32).start()
            return carry

        lax.fori_loop(1, 16, send_d1, 0)
        some = d1.at[pl.ds(0, 15)]
        expect("d1", some)
        expect("d1.send", some)
        out_block[k] = prod[k]
        need("d1")
        d1_sum[...] = jnp.sum(d1[...], axis=0) + own_sq[...]
        d2[k, r] = d1_sum[...]

        def send_d2(j, carry):
            remote(d1_sum, d2.at[k, r], sem("d2.send"), sem("d2"), (r + j) % 8, c).start()
            remote(d1_sum, d2.at[k, r], sem("d2.send"), sem("d2"), (r + j) % 8, col(z, xl, 1 - k)).start()
            return carry

        lax.fori_loop(1, 8, send_d2, 0)
        remote(d1_sum, d2.at[k, r], sem("d2.send"), sem("d2"), r, col(z, xl, 1 - k)).start()
        expect("d2", some)
        expect("d2.send", some)
        need("d2")
        for s in range(2):
            out_diag[pl.ds(s, 1), :] = jnp.sum(d2[s], axis=0)

    body()
    need(*pending)


def per_device(ancestor, panel, factor_inv, pattern):
    vmem = pltpu.VMEM
    block, diag = pl.pallas_call(
        kernel,
        out_shape=(jax.ShapeDtypeStruct((2, 16, 512), F32), jax.ShapeDtypeStruct((2, 512), F32)),
        in_specs=[pl.BlockSpec(memory_space=pl.ANY)] * 4,
        out_specs=(pl.BlockSpec(memory_space=vmem), pl.BlockSpec(memory_space=vmem)),
        scratch_shapes=[
            pltpu.SMEM((2, 16), jnp.int32),
            pltpu.SMEM((16,), jnp.int32),
            vmem((16, 8, 256), F32),
            vmem((8, 2, 8, 256), F32),
            vmem((2, 2, 4, 32, 256), F32),
            vmem((4, 512, 128), F32),
            vmem((4, 2, 64, 512), F32),
            vmem((8, 8, 256), F32),
            vmem((16, 32, 256), F32),
            vmem((2, 5, 32, 256), F32),
            vmem((2, 2, 32, 256), F32),
            vmem((2, 2, 32, 128), F32),
            vmem((2, 32, 256), F32),
            vmem((32, 512), F32),
            vmem((2, 16, 512), F32),
            vmem((1, 512), F32),
            vmem((1, 512), F32),
            vmem((16, 1, 512), F32),
            vmem((1, 512), F32),
            vmem((2, 8, 1, 512), F32),
            vmem((512, 512), BF16),
            vmem((512, 512), BF16),
            vmem((512, 512), BF16),
            vmem((512, 512), BF16),
            pltpu.SemaphoreType.DMA((48,)),
            pltpu.SemaphoreType.DMA((8,)),
            pltpu.SemaphoreType.DMA((2, 2, 2)),
        ],
        compiler_params=pltpu.CompilerParams(
            collective_id=0, has_side_effects=True, vmem_limit_bytes=32 * 1024 * 1024
        ),
    )(*[pltpu.with_memory_space_constraint(x, pltpu.HBM) for x in (ancestor, panel, factor_inv, pattern)])
    return block, diag


def solution(mesh):
    in_specs = (P(None, "row", "col"), P(None, "col", None), P(None, "row", None), P())
    out_specs = (P(None, ("row", "col"), None), P())
    return jax.shard_map(per_device, mesh=mesh, in_specs=in_specs, out_specs=out_specs, check_vma=False)
```

```python
import jax
import jax.numpy as jnp
from jax import lax
from jax.experimental import pallas as pl
from jax.experimental.pallas import tpu as pltpu
from jax.sharding import PartitionSpec as P


MESH = pl.DeviceIdType.MESH
F32 = jnp.float32
BF16 = jnp.bfloat16


def halves(x):
    high = x.astype(BF16)
    low = (x - high.astype(F32)).astype(BF16)
    return high, low


def dot3(a_high, a_low, b_high, b_low):
    def dot(a, b):
        return jnp.dot(a, b, preferred_element_type=F32)

    return dot(a_high, b_high) + (dot(a_low, b_high) + dot(a_high, b_low))


def times_factor(x, f_high, f_low):
    high, low = halves(x)
    both = jnp.concatenate([high, low], axis=0)
    n = x.shape[0]

    def part(first, cols):
        rows = slice(first, 512)
        twice = jnp.dot(both[:, rows], f_high[rows, cols], preferred_element_type=F32)
        return twice[:n] + (twice[n:] + jnp.dot(high[:, rows], f_low[rows, cols], preferred_element_type=F32))

    return jnp.concatenate([part(0, slice(0, 256)), part(256, slice(256, 512))], axis=1)


def kernel(
    anc, pan, fin, pat_hbm, out_block, out_diag,
    pat, inv, buf_a, send_b, send_p, pbuf, abuf, fbuf, cbuf, rbuf, relay3, relay4, pdiag, spread, prod, d_send, own_sq,
    d1, d1_sum, d2, diag, a_high, a_low, f_high, f_low, sems, b_sems, relay_sems,
):
    r = lax.axis_index("row")
    c = lax.axis_index("col")
    y, xh = r // 2, r % 2
    z, xl, k = c // 4, (c // 2) % 2, c % 2
    q = 2 * z + xl

    names = {}
    pending = {}

    def sem(name):
        return sems.at[names.setdefault(name, len(names))]

    def col(z_, xl_, k_):
        return z_ * 4 + xl_ * 2 + k_

    def remote(src, dst, send_sem, recv_sem, row_, col_):
        return pltpu.make_async_remote_copy(
            src_ref=src, dst_ref=dst, send_sem=send_sem, recv_sem=recv_sem, device_id=(row_, col_), device_id_type=MESH
        )

    def wait_bytes(ref, s):
        pltpu.make_async_copy(ref, ref, s).wait()

    def expect(name, ref):
        pending[name] = lambda: wait_bytes(ref, sem(name))

    def need(*keys):
        for key in keys:
            pending.pop(key)()

    def send(name, src, dst, row_, col_, arrives):
        copy = remote(src, dst, sem(name + ".send"), sem(name), row_, col_)
        copy.start()
        pending[name + ".send"] = copy.wait_send
        if arrives is not None:
            expect(name, arrives)

    barrier = pltpu.get_barrier_semaphore()

    def greet(row_, col_):
        pl.semaphore_signal(barrier, inc=1, device_id=(row_, col_), device_id_type=MESH)

    def piece(zi, xi):
        return pan.at[:, pl.ds(pl.multiple_of(32 * y + 8 * (zi % 4), 8), 8), pl.ds(pl.multiple_of(256 * xi, 256), 256)]

    quarter = abuf.at[:, 2 * xl + k]

    @pl.when(k == 0)
    def _():
        greet(r, c + 1)
        pl.semaphore_wait(barrier, 16)

        def send_a(j, carry):
            zi, xi = (z + 3 - j // 2) % 4, (xl + j + 1) % 2
            remote(piece(zi, xi), buf_a.at[q], sem("a.send"), sem("a"), r, col(zi, xi, 1)).start()
            return carry

        lax.fori_loop(0, 8, send_a, 0)
        anc_x = remote(anc, quarter, sem("anc_x"), sem("anc"), r, col(z, 1 - xl, 1))
        anc_x.start()
        anc_core = remote(anc, quarter, sem("anc_core"), sem("anc"), r, c + 1)
        anc_core.start()
        wait_bytes(buf_a.at[pl.ds(0, 8)], sem("a.send"))
        anc_x.wait_send()
        anc_core.wait_send()
        wait_bytes(out_block, sem("o"))
        wait_bytes(out_diag, sem("diag"))

    def body():
        pat_copy = pltpu.make_async_copy(pat_hbm, pat, sem("pat"))
        pat_copy.start()
        pending["pat"] = pat_copy.wait

        def greet_col(j, carry):
            half = j // 2
            other = (c + 16 + jnp.where(j % 2 == 0, half, 32 - half)) % 32
            greet(r, other)
            return carry

        lax.fori_loop(1, 32, greet_col, 0)
        for d in (2, 1, 3):
            greet(2 * ((y + d) % 4) + xh, c)
        greet(2 * y + 1 - xh, col(z, 1 - xl, k))
        pl.semaphore_wait(barrier, 15 + 3 + 1 + 1)

        def send_a(j, carry):
            zi, xi = 4 + (z + j // 2) % 4, (xl + j) % 2
            remote(piece(zi, xi), buf_a.at[q], sem("a.send"), sem("a"), r, col(zi, xi, 1)).start()
            return carry

        lax.fori_loop(1, 8, send_a, 0)

        @pl.when(z >= 4)
        def _():
            pltpu.make_async_copy(piece(z, xl), buf_a.at[q], sem("a")).start()

        @pl.when(z < 4)
        def _():
            remote(piece(4 + z, xl), buf_a.at[q], sem("a.send"), sem("a"), r, col(4 + z, xl, 1)).start()

        expect("a", buf_a)

        def wait_send_a():
            pl.when(z >= 4)(lambda: wait_bytes(buf_a.at[pl.ds(0, 7)], sem("a.send")))
            pl.when(z < 4)(lambda: wait_bytes(buf_a.at[pl.ds(0, 8)], sem("a.send")))

        pending["a.send"] = wait_send_a

        own = fbuf.at[:, y, xh]
        f_own = pltpu.make_async_copy(fin, own, sem("f_own"))
        f_own.start()
        pending["f_own"] = f_own.wait
        for d in (2, 1, 3):
            send("f%d" % d, fin, own, 2 * ((y + d) % 4) + xh, c, fbuf.at[:, (y + 4 - d) % 4, xh])

        pltpu.make_async_copy(anc, quarter, sem("anc")).start()
        anc_x = remote(anc, quarter, sem("anc_x"), sem("anc"), r, col(z, 1 - xl, 1))
        anc_x.start()
        pending["anc_x"] = anc_x.wait_send
        expect("anc", abuf)

        need("pat")

        def invert(n, carry):
            for s in range(2):
                found = jnp.int32(0)
                for j in range(16):
                    found = jnp.where(pat[s, j] == n, jnp.int32(j), found)
                inv[s, n] = found
            return carry

        lax.fori_loop(0, 16, invert, 0)
        need("a")

        def b_place(zi):
            return pbuf.at[:, :, zi // 4, y, pl.ds(pl.multiple_of(8 * (zi % 4), 8), 8), :]

        def choose(zd):
            for s in range(2):
                for t in range(2):
                    send_b[zd, s, t] = buf_a[inv[s, 2 * zd + t], s]

        def near_first(j):
            half = j // 2 + 1
            return jnp.where(j % 2 == 0, half, 8 - half)

        def send_b_to(j, carry):
            d = near_first(j)
            zd = (z + d) % 8
            choose(zd)
            remote(send_b.at[zd], b_place(z), sem("b.send"), b_sems.at[d], r, col(zd, xl, k)).start()
            return carry

        choose(z)
        pltpu.make_async_copy(send_b.at[z], b_place(z), b_sems.at[0]).start()
        lax.fori_loop(0, 7, send_b_to, 0)
        expect("b.send", send_b.at[pl.ds(0, 7)])

        need("f_own", "f1", "f2", "f3")
        send("f_x", fbuf.at[:, :, xh], fbuf.at[:, :, xh], 2 * y + 1 - xh, col(z, 1 - xl, k), fbuf.at[:, :, 1 - xh])

        pd_to, pd_x = 2 * (z // 4) + y // 2, y % 2
        pd_self = jnp.logical_and(z % 4 == pd_to, xl == pd_x)

        def send_pd(j, carry):
            yd, t = (y + j // 2) % 4, j % 2
            for s in range(2):
                send_p[j, s] = buf_a[inv[s, 2 * (2 * yd + xh) + t], s]
            place = pdiag.at[:, xl, pl.ds(pl.multiple_of(8 * (z % 4), 8), 8), :]
            to_row, to_col = 2 * yd + xh, col(pd_to + 4 * t, pd_x, k)

            def away():
                remote(send_p.at[j], place, sem("pd.send"), sem("pd"), to_row, to_col).start()

            if isinstance(j, int):
                mine = to_col == c
                pl.when(mine)(lambda: pltpu.make_async_copy(send_p.at[j], place, sem("pd")).start())
                pl.when(jnp.logical_not(mine))(away)
            else:
                away()
            return carry

        lax.fori_loop(2, 8, send_pd, 0)
        send_pd(0, 0)
        send_pd(1, 0)
        expect("pd", pdiag)

        def wait_send_pd():
            pl.when(pd_self)(lambda: wait_bytes(send_p.at[pl.ds(0, 7)], sem("pd.send")))
            pl.when(jnp.logical_not(pd_self))(lambda: wait_bytes(send_p, sem("pd.send")))

        pending["pd.send"] = wait_send_pd

        for d in (0, 1, 7, 2, 6, 3, 5, 4):
            place = b_place((z + 8 - d) % 8)
            wait_bytes(place, b_sems.at[d])
            for dy in (2, 1, 3):
                remote(place, place, sem("c.send"), sem("c"), 2 * ((y + dy) % 4) + xh, c).start()
        three = pbuf.at[:, :, :, pl.ds(0, 3)]
        expect("c", three)
        expect("c.send", three)

        need("anc")
        for s in range(2):
            for j in range(4):
                high, low = halves(abuf[s, j])
                a_high[s, :, 128 * j : 128 * j + 128] = high
                a_low[s, :, 128 * j : 128 * j + 128] = low

        need("c")

        ways = ((1, pl.ds(0, 128)), (7, pl.ds(128, 128)))
        xs = ((xl + 1) % 2, xl)
        for s in range(2):
            p_high, p_low = halves(pbuf[s].reshape(512, 256))
            cbuf[s] = dot3(a_high[s], a_low[s], p_high, p_low).reshape(16, 32, 256)
            for i, xd in enumerate(xs):
                for w, (up, half) in enumerate(ways):
                    remote(
                        cbuf.at[s, 2 * ((z + 4) % 8) + xd, :, half], relay4.at[w, i, s],
                        sem("relay.send"), relay_sems.at[w, i, 0], r, col((z + 2 * up) % 8, xl, k),
                    ).start()
                    remote(
                        cbuf.at[s, 2 * ((z + 3 * up) % 8) + xd], relay3.at[w, i, s],
                        sem("relay.send"), relay_sems.at[w, i, 1], r, col((z + up) % 8, xl, k),
                    ).start()
        expect("relay.send", cbuf.at[:, pl.ds(0, 6)])

        def send_sum(zd, xd, slot):
            remote(
                cbuf.at[:, 2 * zd + xd], rbuf.at[xl, slot], sem("sum.send"), sem("sum"), r, col(zd, xd, k)
            ).start()

        for xd in xs:
            for w, (up, half) in enumerate(ways):
                send_sum((z + up) % 8, xd, 1 + w)
        send_sum(z, 1 - xl, 0)
        rbuf[xl, 0] = cbuf[:, q]
        expect("sum", cbuf.at[:, pl.ds(0, 9)])
        expect("sum.send", cbuf.at[:, pl.ds(0, 9)])

        for i, xd in enumerate(xs):
            for w, (up, half) in enumerate(ways):
                wait_bytes(relay4.at[w, i], relay_sems.at[w, i, 0])
                wait_bytes(relay3.at[w, i], relay_sems.at[w, i, 1])
                zd = (z + 2 * up) % 8
                for s in range(2):
                    cbuf[s, 2 * zd + xd] += relay3[w, i, s]
                    cbuf[s, 2 * zd + xd, :, half] += relay4[w, i, s]
                send_sum(zd, xd, 3 + w)

        need("f_x")
        own_rows = fbuf[:, y, xh]
        own_sq[...] = jnp.sum(own_rows * own_rows, axis=1)
        need("pd")
        for s in range(2):
            high, low = halves(fbuf[s].reshape(512, 512))
            f_high[s] = high
            f_low[s] = low
            spread[s] = times_factor(
                jnp.concatenate([pdiag[s, 0], pdiag[s, 1]], axis=1), f_high.at[s], f_low.at[s]
            )
        need("sum")

        for s in range(2):
            total = jnp.concatenate([jnp.sum(rbuf[0, :, s], axis=0), jnp.sum(rbuf[1, :, s], axis=0)], axis=1)
            result = times_factor(total, f_high.at[s], f_low.at[s])
            d_send[s : s + 1, :] = jnp.sum(spread[s] * result, axis=0, keepdims=True)
            prod[:, s] = -result.reshape(2, 16, 512)

        for dz in (4, 3, 5, 2, 6, 1, 7, 0):
            for xd in (1 - xl, xl):
                if dz or xd is not xl:
                    remote(d_send, d1.at[q], sem("d1.send"), sem("d1"), r, col((z + dz) % 8, xd, k)).start()
        expect("d1", d1.at[pl.ds(0, 15)])
        expect("d1.send", d1.at[pl.ds(0, 15)])
        d1[q] = d_send[...]
        send("o", prod.at[0], out_block, r, c - 1, None)
        out_block[...] = prod[1]
        need("d1")
        d1_sum[...] = jnp.sum(d1[...], axis=0) + own_sq[...]
        for dy, flip in ((2, 1), (1, 1), (3, 1), (2, 0), (0, 1), (1, 0), (3, 0)):
            to = 2 * ((y + dy) % 4) + (xh + flip) % 2
            remote(d1_sum, d2.at[r], sem("d2.send"), sem("d2"), to, c).start()
        d2[r] = d1_sum[...]
        expect("d2", d1.at[pl.ds(0, 7)])
        expect("d2.send", d1.at[pl.ds(0, 7)])
        need("d2")
        diag[...] = jnp.sum(d2[...], axis=0)
        send("diag", diag, out_diag, r, c - 1, None)
        out_diag[...] = diag[...]

    @pl.when(k == 1)
    def _():
        body()
        need(*pending)


def per_device(ancestor, panel, factor_inv, pattern):
    vmem = pltpu.VMEM
    inputs = [pltpu.with_memory_space_constraint(x, pltpu.HBM) for x in (ancestor, panel, factor_inv, pattern)]
    return pl.pallas_call(
        kernel,
        out_shape=(jax.ShapeDtypeStruct((2, 16, 512), F32), jax.ShapeDtypeStruct((2, 512), F32)),
        in_specs=[pl.BlockSpec(memory_space=pl.ANY)] * 4,
        out_specs=(pl.BlockSpec(memory_space=vmem), pl.BlockSpec(memory_space=vmem)),
        scratch_shapes=[
            pltpu.SMEM((2, 16), jnp.int32),
            pltpu.SMEM((2, 16), jnp.int32),
            vmem((16, 2, 8, 256), F32),
            vmem((8, 2, 2, 8, 256), F32),
            vmem((8, 2, 8, 256), F32),
            vmem((2, 2, 2, 4, 32, 256), F32),
            vmem((2, 4, 512, 128), F32),
            vmem((2, 4, 2, 64, 512), F32),
            vmem((2, 16, 32, 256), F32),
            vmem((2, 5, 2, 32, 256), F32),
            vmem((2, 2, 2, 32, 256), F32),
            vmem((2, 2, 2, 32, 128), F32),
            vmem((2, 2, 32, 256), F32),
            vmem((2, 32, 512), F32),
            vmem((2, 2, 16, 512), F32),
            vmem((2, 512), F32),
            vmem((2, 512), F32),
            vmem((16, 2, 512), F32),
            vmem((2, 512), F32),
            vmem((8, 2, 512), F32),
            vmem((2, 512), F32),
            vmem((2, 512, 512), BF16),
            vmem((2, 512, 512), BF16),
            vmem((2, 512, 512), BF16),
            vmem((2, 512, 512), BF16),
            pltpu.SemaphoreType.DMA((40,)),
            pltpu.SemaphoreType.DMA((8,)),
            pltpu.SemaphoreType.DMA((2, 2, 2)),
        ],
        compiler_params=pltpu.CompilerParams(
            collective_id=0, has_side_effects=True, vmem_limit_bytes=32 * 1024 * 1024
        ),
    )(*inputs)


def solution(mesh):
    in_specs = (P(None, "row", "col"), P(None, "col", None), P(None, "row", None), P())
    out_specs = (P(None, ("row", "col"), None), P())
    return jax.shard_map(per_device, mesh=mesh, in_specs=in_specs, out_specs=out_specs, check_vma=False)
```

```python
import jax
import jax.numpy as jnp
from jax import lax
from jax.experimental import pallas as pl
from jax.experimental.pallas import tpu as pltpu
from jax.sharding import PartitionSpec as P


MESH = pl.DeviceIdType.MESH
F32 = jnp.float32
BF16 = jnp.bfloat16


def halves(x):
    high = x.astype(BF16)
    low = (x - high.astype(F32)).astype(BF16)
    return high, low


def dot3(a_high, a_low, b_high, b_low):
    def dot(a, b):
        return jnp.dot(a, b, preferred_element_type=F32)

    return dot(a_high, b_high) + (dot(a_low, b_high) + dot(a_high, b_low))


def times_factor(x, f_high, f_low):
    high, low = halves(x)
    both = jnp.concatenate([high, low], axis=0)
    n = x.shape[0]

    def part(first, cols):
        rows = slice(first, 512)
        twice = jnp.dot(both[:, rows], f_high[rows, cols], preferred_element_type=F32)
        return twice[:n] + (twice[n:] + jnp.dot(high[:, rows], f_low[rows, cols], preferred_element_type=F32))

    return jnp.concatenate([part(0, slice(0, 256)), part(256, slice(256, 512))], axis=1)


def kernel(
    anc, pan, fin, pat_hbm, out_block, out_diag,
    pat, inv, buf_a, send_b, send_p, pbuf, abuf, fbuf, cbuf, rbuf, relay3, relay4, pdiag, spread, prod, d_send, own_sq,
    d1, d1_sum, d2, diag, a_high, a_low, f_high, f_low, sems, b_sems, relay_sems,
):
    r = lax.axis_index("row")
    c = lax.axis_index("col")
    y, xh = r // 2, r % 2
    z, xl, k = c // 4, (c // 2) % 2, c % 2
    q = 2 * z + xl

    names = {}
    pending = {}

    def sem(name):
        return sems.at[names.setdefault(name, len(names))]

    def col(z_, xl_, k_):
        return z_ * 4 + xl_ * 2 + k_

    def remote(src, dst, send_sem, recv_sem, row_, col_):
        return pltpu.make_async_remote_copy(
            src_ref=src, dst_ref=dst, send_sem=send_sem, recv_sem=recv_sem, device_id=(row_, col_), device_id_type=MESH
        )

    def wait_bytes(ref, s):
        pltpu.make_async_copy(ref, ref, s).wait()

    def expect(name, ref):
        pending[name] = lambda: wait_bytes(ref, sem(name))

    def need(*keys):
        for key in keys:
            pending.pop(key)()

    def send(name, src, dst, row_, col_, arrives):
        copy = remote(src, dst, sem(name + ".send"), sem(name), row_, col_)
        copy.start()
        pending[name + ".send"] = copy.wait_send
        if arrives is not None:
            expect(name, arrives)

    barrier = pltpu.get_barrier_semaphore()

    def greet(row_, col_):
        pl.semaphore_signal(barrier, inc=1, device_id=(row_, col_), device_id_type=MESH)

    def piece(zi, xi):
        return pan.at[:, pl.ds(pl.multiple_of(32 * (zi % 4) + 8 * y, 8), 8), pl.ds(pl.multiple_of(256 * xi, 256), 256)]

    quarter = abuf.at[:, 2 * xl + k]

    @pl.when(k == 0)
    def _():
        greet(r, c + 1)
        pl.semaphore_wait(barrier, 16)

        def send_a(j, carry):
            zi, xi = (z + 3 - j // 2) % 4, (xl + j + 1) % 2
            remote(piece(zi, xi), buf_a.at[q], sem("a.send"), sem("a"), r, col(zi, xi, 1)).start()
            return carry

        lax.fori_loop(0, 8, send_a, 0)
        anc_x = remote(anc, quarter, sem("anc_x"), sem("anc"), r, col(z, 1 - xl, 1))
        anc_x.start()
        anc_core = remote(anc, quarter, sem("anc_core"), sem("anc"), r, c + 1)
        anc_core.start()
        wait_bytes(buf_a.at[pl.ds(0, 8)], sem("a.send"))
        anc_x.wait_send()
        anc_core.wait_send()
        wait_bytes(out_block, sem("o"))
        wait_bytes(out_diag, sem("diag"))

    def body():
        pat_copy = pltpu.make_async_copy(pat_hbm, pat, sem("pat"))
        pat_copy.start()
        pending["pat"] = pat_copy.wait

        def greet_col(j, carry):
            half = j // 2
            other = (c + 16 + jnp.where(j % 2 == 0, half, 32 - half)) % 32
            greet(r, other)
            return carry

        lax.fori_loop(1, 32, greet_col, 0)
        for d in (2, 1, 3):
            greet(2 * ((y + d) % 4) + xh, c)
        greet(2 * y + 1 - xh, col(z, 1 - xl, k))
        pl.semaphore_wait(barrier, 15 + 3 + 1 + 1)

        def send_a(j, carry):
            zi, xi = 4 + (z + j // 2) % 4, (xl + j) % 2
            remote(piece(zi, xi), buf_a.at[q], sem("a.send"), sem("a"), r, col(zi, xi, 1)).start()
            return carry

        lax.fori_loop(1, 8, send_a, 0)

        @pl.when(z >= 4)
        def _():
            pltpu.make_async_copy(piece(z, xl), buf_a.at[q], sem("a")).start()

        @pl.when(z < 4)
        def _():
            remote(piece(4 + z, xl), buf_a.at[q], sem("a.send"), sem("a"), r, col(4 + z, xl, 1)).start()

        expect("a", buf_a)

        def wait_send_a():
            pl.when(z >= 4)(lambda: wait_bytes(buf_a.at[pl.ds(0, 7)], sem("a.send")))
            pl.when(z < 4)(lambda: wait_bytes(buf_a.at[pl.ds(0, 8)], sem("a.send")))

        pending["a.send"] = wait_send_a

        own = fbuf.at[:, y, xh]
        f_own = pltpu.make_async_copy(fin, own, sem("f_own"))
        f_own.start()
        pending["f_own"] = f_own.wait
        for d in (2, 1, 3):
            send("f%d" % d, fin, own, 2 * ((y + d) % 4) + xh, c, fbuf.at[:, (y + 4 - d) % 4, xh])

        pltpu.make_async_copy(anc, quarter, sem("anc")).start()
        anc_x = remote(anc, quarter, sem("anc_x"), sem("anc"), r, col(z, 1 - xl, 1))
        anc_x.start()
        pending["anc_x"] = anc_x.wait_send
        expect("anc", abuf)

        need("pat")

        def invert(n, carry):
            for s in range(2):
                found = jnp.int32(0)
                for j in range(16):
                    found = jnp.where(pat[s, j] == n, jnp.int32(j), found)
                inv[s, n] = found
            return carry

        lax.fori_loop(0, 16, invert, 0)
        need("a")

        def b_place(zi):
            return pbuf.at[:, :, zi, y]

        def choose(zd):
            for s in range(2):
                for t in range(2):
                    send_b[zd, s, t] = buf_a[inv[s, 2 * zd + t], s]

        def near_first(j):
            half = j // 2 + 1
            return jnp.where(j % 2 == 0, half, 8 - half)

        def send_b_to(j, carry):
            d = near_first(j)
            zd = (z + d) % 8
            choose(zd)
            remote(send_b.at[zd], b_place(z), sem("b.send"), b_sems.at[d], r, col(zd, xl, k)).start()
            return carry

        choose(z)
        pltpu.make_async_copy(send_b.at[z], b_place(z), b_sems.at[0]).start()
        lax.fori_loop(0, 7, send_b_to, 0)
        expect("b.send", send_b.at[pl.ds(0, 7)])

        need("f_own", "f1", "f2", "f3")
        send("f_x", fbuf.at[:, :, xh], fbuf.at[:, :, xh], 2 * y + 1 - xh, col(z, 1 - xl, k), fbuf.at[:, :, 1 - xh])

        for d in (0, 1, 7, 2, 6, 3, 5, 4):
            place = b_place((z + 8 - d) % 8)
            wait_bytes(place, b_sems.at[d])
            for dy in (2, 1, 3):
                remote(place, place, sem("c.send"), sem("c"), 2 * ((y + dy) % 4) + xh, c).start()
        three = pbuf.at[:, :, :, pl.ds(0, 3)]
        expect("c", three)
        expect("c.send", three)
        pd_to, pd_x = z // 2, z % 2
        pd_self = jnp.logical_and(jnp.logical_or(pd_to == z, pd_to + 4 == z), xl == pd_x)

        def send_pd(j, carry):
            yd, t = (y + j // 2) % 4, j % 2
            for s in range(2):
                send_p[j, s] = buf_a[inv[s, 2 * (2 * yd + xh) + t], s]
            place = pdiag.at[:, xl, pl.ds(pl.multiple_of(8 * y, 8), 8), :]
            to_row, to_col = 2 * yd + xh, col(pd_to + 4 * t, pd_x, k)

            def away():
                remote(send_p.at[j], place, sem("pd.send"), sem("pd"), to_row, to_col).start()

            if isinstance(j, int):
                mine = to_col == c
                pl.when(mine)(lambda: pltpu.make_async_copy(send_p.at[j], place, sem("pd")).start())
                pl.when(jnp.logical_not(mine))(away)
            else:
                away()
            return carry

        lax.fori_loop(2, 8, send_pd, 0)
        send_pd(0, 0)
        send_pd(1, 0)
        expect("pd", pdiag)

        def wait_send_pd():
            pl.when(pd_self)(lambda: wait_bytes(send_p.at[pl.ds(0, 7)], sem("pd.send")))
            pl.when(jnp.logical_not(pd_self))(lambda: wait_bytes(send_p, sem("pd.send")))

        pending["pd.send"] = wait_send_pd


        need("anc")
        for s in range(2):
            for j in range(4):
                high, low = halves(abuf[s, j])
                a_high[s, :, 128 * j : 128 * j + 128] = high
                a_low[s, :, 128 * j : 128 * j + 128] = low

        need("c")

        ways = ((1, pl.ds(0, 128)), (7, pl.ds(128, 128)))
        xs = ((xl + 1) % 2, xl)
        for s in range(2):
            p_high, p_low = halves(pbuf[s].reshape(512, 256))
            cbuf[s] = dot3(a_high[s], a_low[s], p_high, p_low).reshape(16, 32, 256)
            for i, xd in enumerate(xs):
                for w, (up, half) in enumerate(ways):
                    remote(
                        cbuf.at[s, 2 * ((z + 4) % 8) + xd, :, half], relay4.at[w, i, s],
                        sem("relay.send"), relay_sems.at[w, i, 0], r, col((z + 2 * up) % 8, xl, k),
                    ).start()
                    remote(
                        cbuf.at[s, 2 * ((z + 3 * up) % 8) + xd], relay3.at[w, i, s],
                        sem("relay.send"), relay_sems.at[w, i, 1], r, col((z + up) % 8, xl, k),
                    ).start()
        expect("relay.send", cbuf.at[:, pl.ds(0, 6)])

        def send_sum(zd, xd, slot):
            remote(
                cbuf.at[:, 2 * zd + xd], rbuf.at[xl, slot], sem("sum.send"), sem("sum"), r, col(zd, xd, k)
            ).start()

        for xd in xs:
            for w, (up, half) in enumerate(ways):
                send_sum((z + up) % 8, xd, 1 + w)
        send_sum(z, 1 - xl, 0)
        rbuf[xl, 0] = cbuf[:, q]
        expect("sum", cbuf.at[:, pl.ds(0, 9)])
        expect("sum.send", cbuf.at[:, pl.ds(0, 9)])

        for i, xd in enumerate(xs):
            for w, (up, half) in enumerate(ways):
                wait_bytes(relay4.at[w, i], relay_sems.at[w, i, 0])
                wait_bytes(relay3.at[w, i], relay_sems.at[w, i, 1])
                zd = (z + 2 * up) % 8
                for s in range(2):
                    cbuf[s, 2 * zd + xd] += relay3[w, i, s]
                    cbuf[s, 2 * zd + xd, :, half] += relay4[w, i, s]
                send_sum(zd, xd, 3 + w)

        need("f_x")
        own_rows = fbuf[:, y, xh]
        own_sq[...] = jnp.sum(own_rows * own_rows, axis=1)
        need("pd")
        for s in range(2):
            high, low = halves(fbuf[s].reshape(512, 512))
            f_high[s] = high
            f_low[s] = low
            spread[s] = times_factor(
                jnp.concatenate([pdiag[s, 0], pdiag[s, 1]], axis=1), f_high.at[s], f_low.at[s]
            )
        need("sum")

        for s in range(2):
            total = jnp.concatenate([jnp.sum(rbuf[0, :, s], axis=0), jnp.sum(rbuf[1, :, s], axis=0)], axis=1)
            result = times_factor(total, f_high.at[s], f_low.at[s])
            d_send[s : s + 1, :] = jnp.sum(spread[s] * result, axis=0, keepdims=True)
            prod[:, s] = -result.reshape(2, 16, 512)

        for dz in (4, 3, 5, 2, 6, 1, 7, 0):
            for xd in (1 - xl, xl):
                if dz or xd is not xl:
                    remote(d_send, d1.at[q], sem("d1.send"), sem("d1"), r, col((z + dz) % 8, xd, k)).start()
        expect("d1", d1.at[pl.ds(0, 15)])
        expect("d1.send", d1.at[pl.ds(0, 15)])
        d1[q] = d_send[...]
        send("o", prod.at[0], out_block, r, c - 1, None)
        out_block[...] = prod[1]
        need("d1")
        d1_sum[...] = jnp.sum(d1[...], axis=0) + own_sq[...]
        for dy, flip in ((2, 1), (1, 1), (3, 1), (2, 0), (0, 1), (1, 0), (3, 0)):
            to = 2 * ((y + dy) % 4) + (xh + flip) % 2
            remote(d1_sum, d2.at[r], sem("d2.send"), sem("d2"), to, c).start()
        d2[r] = d1_sum[...]
        expect("d2", d1.at[pl.ds(0, 7)])
        expect("d2.send", d1.at[pl.ds(0, 7)])
        need("d2")
        diag[...] = jnp.sum(d2[...], axis=0)
        send("diag", diag, out_diag, r, c - 1, None)
        out_diag[...] = diag[...]

    @pl.when(k == 1)
    def _():
        body()
        need(*pending)


def per_device(ancestor, panel, factor_inv, pattern):
    vmem = pltpu.VMEM
    inputs = [pltpu.with_memory_space_constraint(x, pltpu.HBM) for x in (ancestor, panel, factor_inv, pattern)]
    return pl.pallas_call(
        kernel,
        out_shape=(jax.ShapeDtypeStruct((2, 16, 512), F32), jax.ShapeDtypeStruct((2, 512), F32)),
        in_specs=[pl.BlockSpec(memory_space=pl.ANY)] * 4,
        out_specs=(pl.BlockSpec(memory_space=vmem), pl.BlockSpec(memory_space=vmem)),
        scratch_shapes=[
            pltpu.SMEM((2, 16), jnp.int32),
            pltpu.SMEM((2, 16), jnp.int32),
            vmem((16, 2, 8, 256), F32),
            vmem((8, 2, 2, 8, 256), F32),
            vmem((8, 2, 8, 256), F32),
            vmem((2, 2, 8, 4, 8, 256), F32),
            vmem((2, 4, 512, 128), F32),
            vmem((2, 4, 2, 64, 512), F32),
            vmem((2, 16, 32, 256), F32),
            vmem((2, 5, 2, 32, 256), F32),
            vmem((2, 2, 2, 32, 256), F32),
            vmem((2, 2, 2, 32, 128), F32),
            vmem((2, 2, 32, 256), F32),
            vmem((2, 32, 512), F32),
            vmem((2, 2, 16, 512), F32),
            vmem((2, 512), F32),
            vmem((2, 512), F32),
            vmem((16, 2, 512), F32),
            vmem((2, 512), F32),
            vmem((8, 2, 512), F32),
            vmem((2, 512), F32),
            vmem((2, 512, 512), BF16),
            vmem((2, 512, 512), BF16),
            vmem((2, 512, 512), BF16),
            vmem((2, 512, 512), BF16),
            pltpu.SemaphoreType.DMA((40,)),
            pltpu.SemaphoreType.DMA((8,)),
            pltpu.SemaphoreType.DMA((2, 2, 2)),
        ],
        compiler_params=pltpu.CompilerParams(
            collective_id=0, has_side_effects=True, vmem_limit_bytes=32 * 1024 * 1024
        ),
    )(*inputs)


def solution(mesh):
    in_specs = (P(None, "row", "col"), P(None, "col", None), P(None, "row", None), P())
    out_specs = (P(None, ("row", "col"), None), P())
    return jax.shard_map(per_device, mesh=mesh, in_specs=in_specs, out_specs=out_specs, check_vma=False)
```

```python
import jax
import jax.numpy as jnp
from jax import lax
from jax.experimental import pallas as pl
from jax.experimental.pallas import tpu as pltpu
from jax.sharding import PartitionSpec as P


MESH = pl.DeviceIdType.MESH
F32 = jnp.float32
BF16 = jnp.bfloat16


def halves(x):
    high = x.astype(BF16)
    low = (x - high.astype(F32)).astype(BF16)
    return high, low


def dot3(a_high, a_low, b_high, b_low):
    def dot(a, b):
        return jnp.dot(a, b, preferred_element_type=F32)

    return dot(a_high, b_high) + (dot(a_low, b_high) + dot(a_high, b_low))


def times_factor(x, f_high, f_low):
    high, low = halves(x)
    both = jnp.concatenate([high, low], axis=0)
    n = x.shape[0]

    def part(first, cols):
        rows = slice(first, 512)
        twice = jnp.dot(both[:, rows], f_high[rows, cols], preferred_element_type=F32)
        return twice[:n] + (twice[n:] + jnp.dot(high[:, rows], f_low[rows, cols], preferred_element_type=F32))

    return jnp.concatenate([part(0, slice(0, 256)), part(256, slice(256, 512))], axis=1)


def kernel(
    anc, pan, fin, pat_hbm, out_block, out_diag,
    pat, inv, buf_a, send_b, send_p, pbuf, abuf, fbuf, cbuf, rbuf, relay3, relay4, pdiag, spread, prod, d_send, own_sq,
    d1, d1_sum, d2, a_high, a_low, f_high, f_low, sems, b_sems, relay_sems,
):
    r = lax.axis_index("row")
    c = lax.axis_index("col")
    y, xh = r // 2, r % 2
    z, xl, k = c // 4, (c // 2) % 2, c % 2
    q = 2 * z + xl

    names = {}
    pending = {}

    def sem(name):
        return sems.at[names.setdefault(name, len(names))]

    def col(z_, xl_, k_):
        return z_ * 4 + xl_ * 2 + k_

    def remote(src, dst, send_sem, recv_sem, row_, col_):
        return pltpu.make_async_remote_copy(
            src_ref=src, dst_ref=dst, send_sem=send_sem, recv_sem=recv_sem, device_id=(row_, col_), device_id_type=MESH
        )

    def wait_bytes(ref, s):
        pltpu.make_async_copy(ref, ref, s).wait()

    def expect(name, ref):
        pending[name] = lambda: wait_bytes(ref, sem(name))

    def need(*keys):
        for key in keys:
            pending.pop(key)()

    def send(name, src, dst, row_, col_, arrives):
        copy = remote(src, dst, sem(name + ".send"), sem(name), row_, col_)
        copy.start()
        pending[name + ".send"] = copy.wait_send
        if arrives is not None:
            expect(name, arrives)

    barrier = pltpu.get_barrier_semaphore()

    def greet(row_, col_):
        pl.semaphore_signal(barrier, inc=1, device_id=(row_, col_), device_id_type=MESH)

    def piece(zi, xi):
        return pan.at[:, pl.ds(pl.multiple_of(32 * (zi % 4) + 8 * y, 8), 8), pl.ds(pl.multiple_of(256 * xi, 256), 256)]

    quarter = abuf.at[:, 2 * xl + k]

    @pl.when(k == 0)
    def _():
        def greet_row(j, carry):
            greet((r + j) % 8, c + 1)
            return carry

        lax.fori_loop(0, 8, greet_row, 0)
        pl.semaphore_wait(barrier, 16)

        def send_a(j, carry):
            zi, xi = (z + 3 - j // 2) % 4, (xl + j + 1) % 2
            remote(piece(zi, xi), buf_a.at[q], sem("a.send"), sem("a"), r, col(zi, xi, 1)).start()
            return carry

        lax.fori_loop(0, 8, send_a, 0)
        anc_x = remote(anc, quarter, sem("anc_x"), sem("anc"), r, col(z, 1 - xl, 1))
        anc_x.start()
        anc_core = remote(anc, quarter, sem("anc_core"), sem("anc"), r, c + 1)
        anc_core.start()
        wait_bytes(buf_a.at[pl.ds(0, 8)], sem("a.send"))
        anc_x.wait_send()
        anc_core.wait_send()
        wait_bytes(out_block, sem("o"))
        wait_bytes(d2, sem("d2"))
        out_diag[...] = jnp.sum(d2[...], axis=0)

    def body():
        pat_copy = pltpu.make_async_copy(pat_hbm, pat, sem("pat"))
        pat_copy.start()
        pending["pat"] = pat_copy.wait

        def greet_col(j, carry):
            half = j // 2
            other = (c + 16 + jnp.where(j % 2 == 0, half, 32 - half)) % 32
            greet(r, other)
            return carry

        lax.fori_loop(1, 32, greet_col, 0)
        for d in (2, 1, 3):
            greet(2 * ((y + d) % 4) + xh, c)
        greet(2 * y + 1 - xh, col(z, 1 - xl, k))
        pl.semaphore_wait(barrier, 15 + 3 + 1 + 8)

        def send_a(j, carry):
            zi, xi = 4 + (z + j // 2) % 4, (xl + j) % 2
            remote(piece(zi, xi), buf_a.at[q], sem("a.send"), sem("a"), r, col(zi, xi, 1)).start()
            return carry

        lax.fori_loop(1, 8, send_a, 0)

        @pl.when(z >= 4)
        def _():
            pltpu.make_async_copy(piece(z, xl), buf_a.at[q], sem("a")).start()

        @pl.when(z < 4)
        def _():
            remote(piece(4 + z, xl), buf_a.at[q], sem("a.send"), sem("a"), r, col(4 + z, xl, 1)).start()

        expect("a", buf_a)

        def wait_send_a():
            pl.when(z >= 4)(lambda: wait_bytes(buf_a.at[pl.ds(0, 7)], sem("a.send")))
            pl.when(z < 4)(lambda: wait_bytes(buf_a.at[pl.ds(0, 8)], sem("a.send")))

        pending["a.send"] = wait_send_a

        own = fbuf.at[:, y, xh]
        f_own = pltpu.make_async_copy(fin, own, sem("f_own"))
        f_own.start()
        pending["f_own"] = f_own.wait
        for d in (2, 1, 3):
            send("f%d" % d, fin, own, 2 * ((y + d) % 4) + xh, c, fbuf.at[:, (y + 4 - d) % 4, xh])

        pltpu.make_async_copy(anc, quarter, sem("anc")).start()
        anc_x = remote(anc, quarter, sem("anc_x"), sem("anc"), r, col(z, 1 - xl, 1))
        anc_x.start()
        pending["anc_x"] = anc_x.wait_send
        expect("anc", abuf)

        need("pat")

        def invert(n, carry):
            for s in range(2):
                found = jnp.int32(0)
                for j in range(16):
                    found = jnp.where(pat[s, j] == n, jnp.int32(j), found)
                inv[s, n] = found
            return carry

        lax.fori_loop(0, 16, invert, 0)
        need("a")

        def b_place(zi):
            return pbuf.at[:, :, zi, y]

        def choose(zd):
            for s in range(2):
                for t in range(2):
                    send_b[zd, s, t] = buf_a[inv[s, 2 * zd + t], s]

        def near_first(j):
            half = j // 2 + 1
            return jnp.where(j % 2 == 0, half, 8 - half)

        def send_b_to(j, carry):
            d = near_first(j)
            zd = (z + d) % 8
            choose(zd)
            remote(send_b.at[zd], b_place(z), sem("b.send"), b_sems.at[d], r, col(zd, xl, k)).start()
            return carry

        choose(z)
        pltpu.make_async_copy(send_b.at[z], b_place(z), b_sems.at[0]).start()
        lax.fori_loop(0, 7, send_b_to, 0)
        expect("b.send", send_b.at[pl.ds(0, 7)])

        need("f_own", "f1", "f2", "f3")
        for y_ in range(4):
            width = pl.ds(0, 128 * (y_ + 1))
            send(
                "f_x%d" % y_, fbuf.at[:, y_, xh, :, width], fbuf.at[:, y_, xh, :, width],
                2 * y + 1 - xh, col(z, 1 - xl, k), fbuf.at[:, y_, 1 - xh, :, width],
            )

        for d in (0, 1, 7, 2, 6, 3, 5, 4):
            place = b_place((z + 8 - d) % 8)
            wait_bytes(place, b_sems.at[d])
            for dy in (2, 1, 3):
                remote(place, place, sem("c.send"), sem("c"), 2 * ((y + dy) % 4) + xh, c).start()
        three = pbuf.at[:, :, :, pl.ds(0, 3)]
        expect("c", three)
        expect("c.send", three)
        pd_to, pd_x = z // 2, z % 2
        pd_self = jnp.logical_and(jnp.logical_or(pd_to == z, pd_to + 4 == z), xl == pd_x)

        def send_pd(j, carry):
            yd, t = (y + j // 2) % 4, j % 2
            for s in range(2):
                send_p[j, s] = buf_a[inv[s, 2 * (2 * yd + xh) + t], s]
            place = pdiag.at[:, xl, pl.ds(pl.multiple_of(8 * y, 8), 8), :]
            to_row, to_col = 2 * yd + xh, col(pd_to + 4 * t, pd_x, k)

            def away():
                remote(send_p.at[j], place, sem("pd.send"), sem("pd"), to_row, to_col).start()

            if isinstance(j, int):
                mine = to_col == c
                pl.when(mine)(lambda: pltpu.make_async_copy(send_p.at[j], place, sem("pd")).start())
                pl.when(jnp.logical_not(mine))(away)
            else:
                away()
            return carry

        lax.fori_loop(2, 8, send_pd, 0)
        send_pd(0, 0)
        send_pd(1, 0)
        expect("pd", pdiag)

        def wait_send_pd():
            pl.when(pd_self)(lambda: wait_bytes(send_p.at[pl.ds(0, 7)], sem("pd.send")))
            pl.when(jnp.logical_not(pd_self))(lambda: wait_bytes(send_p, sem("pd.send")))

        pending["pd.send"] = wait_send_pd


        need("anc")
        for s in range(2):
            for j in range(4):
                high, low = halves(abuf[s, j])
                a_high[s, :, 128 * j : 128 * j + 128] = high
                a_low[s, :, 128 * j : 128 * j + 128] = low

        need("c")

        ways = ((1, pl.ds(0, 128)), (7, pl.ds(128, 128)))
        xs = ((xl + 1) % 2, xl)
        for s in range(2):
            p_high, p_low = halves(pbuf[s].reshape(512, 256))
            cbuf[s] = dot3(a_high[s], a_low[s], p_high, p_low).reshape(16, 32, 256)
            for i, xd in enumerate(xs):
                for w, (up, half) in enumerate(ways):
                    remote(
                        cbuf.at[s, 2 * ((z + 4) % 8) + xd, :, half], relay4.at[w, i, s],
                        sem("relay.send"), relay_sems.at[w, i, 0], r, col((z + 2 * up) % 8, xl, k),
                    ).start()
                    remote(
                        cbuf.at[s, 2 * ((z + 3 * up) % 8) + xd], relay3.at[w, i, s],
                        sem("relay.send"), relay_sems.at[w, i, 1], r, col((z + up) % 8, xl, k),
                    ).start()
        expect("relay.send", cbuf.at[:, pl.ds(0, 6)])

        def send_sum(zd, xd, slot):
            remote(
                cbuf.at[:, 2 * zd + xd], rbuf.at[xl, slot], sem("sum.send"), sem("sum"), r, col(zd, xd, k)
            ).start()

        for xd in xs:
            for w, (up, half) in enumerate(ways):
                send_sum((z + up) % 8, xd, 1 + w)
        send_sum(z, 1 - xl, 0)
        rbuf[xl, 0] = cbuf[:, q]
        expect("sum", cbuf.at[:, pl.ds(0, 9)])
        expect("sum.send", cbuf.at[:, pl.ds(0, 9)])

        for i, xd in enumerate(xs):
            for w, (up, half) in enumerate(ways):
                wait_bytes(relay4.at[w, i], relay_sems.at[w, i, 0])
                wait_bytes(relay3.at[w, i], relay_sems.at[w, i, 1])
                zd = (z + 2 * up) % 8
                for s in range(2):
                    cbuf[s, 2 * zd + xd] += relay3[w, i, s]
                    cbuf[s, 2 * zd + xd, :, half] += relay4[w, i, s]
                send_sum(zd, xd, 3 + w)

        need("f_x0", "f_x1", "f_x2", "f_x3")
        own_rows = fbuf[:, y, xh]
        own_sq[...] = jnp.sum(own_rows * own_rows, axis=1)
        need("pd")
        for s in range(2):
            for y_ in range(4):
                rows, width = slice(128 * y_, 128 * y_ + 128), 128 * (y_ + 1)
                high, low = halves(fbuf[s, y_, :, :, :width].reshape(128, width))
                f_high[s, rows, :width] = high
                f_low[s, rows, :width] = low
                if y_ % 2 == 0:
                    f_high[s, rows, width : width + 128] = jnp.zeros((128, 128), BF16)
                    f_low[s, rows, width : width + 128] = jnp.zeros((128, 128), BF16)
            spread[s] = times_factor(
                jnp.concatenate([pdiag[s, 0], pdiag[s, 1]], axis=1), f_high.at[s], f_low.at[s]
            )
        need("sum")

        for s in range(2):
            total = jnp.concatenate([jnp.sum(rbuf[0, :, s], axis=0), jnp.sum(rbuf[1, :, s], axis=0)], axis=1)
            result = times_factor(total, f_high.at[s], f_low.at[s])
            d_send[s : s + 1, :] = jnp.sum(spread[s] * result, axis=0, keepdims=True)
            prod[:, s] = -result.reshape(2, 16, 512)

        for dz in (4, 3, 5, 2, 6, 1, 7, 0):
            for xd in (1 - xl, xl):
                if dz or xd is not xl:
                    remote(d_send, d1.at[q], sem("d1.send"), sem("d1"), r, col((z + dz) % 8, xd, k)).start()
        expect("d1", d1.at[pl.ds(0, 15)])
        expect("d1.send", d1.at[pl.ds(0, 15)])
        d1[q] = d_send[...]
        send("o", prod.at[0], out_block, r, c - 1, None)
        out_block[...] = prod[1]
        need("d1")
        d1_sum[...] = jnp.sum(d1[...], axis=0) + own_sq[...]
        for dy, flip in ((2, 1), (1, 1), (3, 1), (2, 0), (0, 1), (1, 0), (3, 0), (0, 0)):
            to = 2 * ((y + dy) % 4) + (xh + flip) % 2
            remote(d1_sum, d2.at[r], sem("d2.send"), sem("d2"), to, c - 1).start()
            if dy or flip:
                remote(d1_sum, d2.at[r], sem("d2.send"), sem("d2"), to, c).start()
        d2[r] = d1_sum[...]
        expect("d2", d1.at[pl.ds(0, 7)])
        expect("d2.send", d1.at[pl.ds(0, 15)])
        need("d2")
        out_diag[...] = jnp.sum(d2[...], axis=0)

    @pl.when(k == 1)
    def _():
        body()
        need(*pending)


def per_device(ancestor, panel, factor_inv, pattern):
    vmem = pltpu.VMEM
    inputs = [pltpu.with_memory_space_constraint(x, pltpu.HBM) for x in (ancestor, panel, factor_inv, pattern)]
    return pl.pallas_call(
        kernel,
        out_shape=(jax.ShapeDtypeStruct((2, 16, 512), F32), jax.ShapeDtypeStruct((2, 512), F32)),
        in_specs=[pl.BlockSpec(memory_space=pl.ANY)] * 4,
        out_specs=(pl.BlockSpec(memory_space=vmem), pl.BlockSpec(memory_space=vmem)),
        scratch_shapes=[
            pltpu.SMEM((2, 16), jnp.int32),
            pltpu.SMEM((2, 16), jnp.int32),
            vmem((16, 2, 8, 256), F32),
            vmem((8, 2, 2, 8, 256), F32),
            vmem((8, 2, 8, 256), F32),
            vmem((2, 2, 8, 4, 8, 256), F32),
            vmem((2, 4, 512, 128), F32),
            vmem((2, 4, 2, 64, 512), F32),
            vmem((2, 16, 32, 256), F32),
            vmem((2, 5, 2, 32, 256), F32),
            vmem((2, 2, 2, 32, 256), F32),
            vmem((2, 2, 2, 32, 128), F32),
            vmem((2, 2, 32, 256), F32),
            vmem((2, 32, 512), F32),
            vmem((2, 2, 16, 512), F32),
            vmem((2, 512), F32),
            vmem((2, 512), F32),
            vmem((16, 2, 512), F32),
            vmem((2, 512), F32),
            vmem((8, 2, 512), F32),
            vmem((2, 512, 512), BF16),
            vmem((2, 512, 512), BF16),
            vmem((2, 512, 512), BF16),
            vmem((2, 512, 512), BF16),
            pltpu.SemaphoreType.DMA((40,)),
            pltpu.SemaphoreType.DMA((8,)),
            pltpu.SemaphoreType.DMA((2, 2, 2)),
        ],
        compiler_params=pltpu.CompilerParams(
            collective_id=0, has_side_effects=True, vmem_limit_bytes=32 * 1024 * 1024
        ),
    )(*inputs)


def solution(mesh):
    in_specs = (P(None, "row", "col"), P(None, "col", None), P(None, "row", None), P())
    out_specs = (P(None, ("row", "col"), None), P())
    return jax.shard_map(per_device, mesh=mesh, in_specs=in_specs, out_specs=out_specs, check_vma=False)
```

```python
import jax
import jax.numpy as jnp
from jax import lax
from jax.experimental import pallas as pl
from jax.experimental.pallas import tpu as pltpu
from jax.sharding import PartitionSpec as P


MESH = pl.DeviceIdType.MESH
F32 = jnp.float32
BF16 = jnp.bfloat16


def halves(x):
    high = x.astype(BF16)
    low = (x - high.astype(F32)).astype(BF16)
    return high, low


def dot3(a_high, a_low, b_high, b_low):
    def dot(a, b):
        return jnp.dot(a, b, preferred_element_type=F32)

    return dot(a_high, b_high) + (dot(a_low, b_high) + dot(a_high, b_low))


def times_factor(x, f_high, f_low):
    high, low = halves(x)
    both = jnp.concatenate([high, low], axis=0)
    n = x.shape[0]

    def part(first, cols):
        rows = slice(first, 512)
        twice = jnp.dot(both[:, rows], f_high[rows, cols], preferred_element_type=F32)
        return twice[:n] + (twice[n:] + jnp.dot(high[:, rows], f_low[rows, cols], preferred_element_type=F32))

    return jnp.concatenate([part(0, slice(0, 256)), part(256, slice(256, 512))], axis=1)


def kernel(
    anc, pan, fin, pat_hbm, out_block, out_diag,
    pat, inv, buf_a, send_b, send_p, pbuf, abuf, fbuf, cbuf, rbuf, relay3, relay4, pdiag, spread, prod, d_send, own_sq,
    d1, d1_sum, d2, a_high, a_low, p_high, p_low, f_high, f_low, sems, b_sems, relay_sems,
):
    r = lax.axis_index("row")
    c = lax.axis_index("col")
    y, xh = r // 2, r % 2
    z, xl, k = c // 4, (c // 2) % 2, c % 2
    q = 2 * z + xl

    names = {}
    pending = {}

    def sem(name):
        return sems.at[names.setdefault(name, len(names))]

    def col(z_, xl_, k_):
        return z_ * 4 + xl_ * 2 + k_

    def remote(src, dst, send_sem, recv_sem, row_, col_):
        return pltpu.make_async_remote_copy(
            src_ref=src, dst_ref=dst, send_sem=send_sem, recv_sem=recv_sem, device_id=(row_, col_), device_id_type=MESH
        )

    def wait_bytes(ref, s):
        pltpu.make_async_copy(ref, ref, s).wait()

    def expect(name, ref):
        pending[name] = lambda: wait_bytes(ref, sem(name))

    def need(*keys):
        for key in keys:
            pending.pop(key)()

    def send(name, src, dst, row_, col_, arrives):
        copy = remote(src, dst, sem(name + ".send"), sem(name), row_, col_)
        copy.start()
        pending[name + ".send"] = copy.wait_send
        if arrives is not None:
            expect(name, arrives)

    barrier = pltpu.get_barrier_semaphore()

    def greet(row_, col_):
        pl.semaphore_signal(barrier, inc=1, device_id=(row_, col_), device_id_type=MESH)

    def piece(zi, xi):
        return pan.at[:, pl.ds(pl.multiple_of(32 * (zi % 4) + 8 * y, 8), 8), pl.ds(pl.multiple_of(256 * xi, 256), 256)]

    quarter = abuf.at[:, 2 * xl + k]

    @pl.when(k == 0)
    def _():
        def greet_row(j, carry):
            greet((r + j) % 8, c + 1)
            return carry

        lax.fori_loop(0, 8, greet_row, 0)
        pl.semaphore_wait(barrier, 16)

        def send_a(j, carry):
            zi, xi = (z + 3 - j // 2) % 4, (xl + j + 1) % 2
            remote(piece(zi, xi), buf_a.at[q], sem("a.send"), sem("a"), r, col(zi, xi, 1)).start()
            return carry

        lax.fori_loop(0, 8, send_a, 0)
        anc_x = remote(anc, quarter, sem("anc_x"), sem("anc"), r, col(z, 1 - xl, 1))
        anc_x.start()
        anc_core = remote(anc, quarter, sem("anc_core"), sem("anc"), r, c + 1)
        anc_core.start()
        wait_bytes(buf_a.at[pl.ds(0, 8)], sem("a.send"))
        anc_x.wait_send()
        anc_core.wait_send()
        wait_bytes(out_block, sem("o"))
        wait_bytes(d2, sem("d2"))
        out_diag[...] = jnp.sum(d2[...], axis=0)

    def body():
        pat_copy = pltpu.make_async_copy(pat_hbm, pat, sem("pat"))
        pat_copy.start()
        pending["pat"] = pat_copy.wait

        def greet_col(j, carry):
            half = j // 2
            other = (c + 16 + jnp.where(j % 2 == 0, half, 32 - half)) % 32
            greet(r, other)
            return carry

        lax.fori_loop(1, 32, greet_col, 0)
        for d in (2, 1, 3):
            greet(2 * ((y + d) % 4) + xh, c)
        greet(2 * y + 1 - xh, col(z, 1 - xl, k))
        pl.semaphore_wait(barrier, 15 + 3 + 1 + 8)

        def send_a(j, carry):
            zi, xi = 4 + (z + j // 2) % 4, (xl + j) % 2
            remote(piece(zi, xi), buf_a.at[q], sem("a.send"), sem("a"), r, col(zi, xi, 1)).start()
            return carry

        lax.fori_loop(1, 8, send_a, 0)

        @pl.when(z >= 4)
        def _():
            pltpu.make_async_copy(piece(z, xl), buf_a.at[q], sem("a")).start()

        @pl.when(z < 4)
        def _():
            remote(piece(4 + z, xl), buf_a.at[q], sem("a.send"), sem("a"), r, col(4 + z, xl, 1)).start()

        expect("a", buf_a)

        def wait_send_a():
            pl.when(z >= 4)(lambda: wait_bytes(buf_a.at[pl.ds(0, 7)], sem("a.send")))
            pl.when(z < 4)(lambda: wait_bytes(buf_a.at[pl.ds(0, 8)], sem("a.send")))

        pending["a.send"] = wait_send_a

        own = fbuf.at[:, y, xh]
        f_own = pltpu.make_async_copy(fin, own, sem("f_own"))
        f_own.start()
        pending["f_own"] = f_own.wait
        for d in (2, 1, 3):
            send("f%d" % d, fin, own, 2 * ((y + d) % 4) + xh, c, fbuf.at[:, (y + 4 - d) % 4, xh])

        pltpu.make_async_copy(anc, quarter, sem("anc")).start()
        anc_x = remote(anc, quarter, sem("anc_x"), sem("anc"), r, col(z, 1 - xl, 1))
        anc_x.start()
        pending["anc_x"] = anc_x.wait_send
        expect("anc", abuf)

        need("pat")

        def invert(n, carry):
            for s in range(2):
                found = jnp.int32(0)
                for j in range(16):
                    found = jnp.where(pat[s, j] == n, jnp.int32(j), found)
                inv[s, n] = found
            return carry

        lax.fori_loop(0, 16, invert, 0)
        need("a")

        def b_place(zi):
            return pbuf.at[:, :, zi, y]

        def choose(zd):
            for s in range(2):
                for t in range(2):
                    send_b[zd, s, t] = buf_a[inv[s, 2 * zd + t], s]

        def near_first(j):
            half = j // 2 + 1
            return jnp.where(j % 2 == 0, half, 8 - half)

        def send_b_to(j, carry):
            d = near_first(j)
            zd = (z + d) % 8
            choose(zd)
            remote(send_b.at[zd], b_place(z), sem("b.send"), b_sems.at[d], r, col(zd, xl, k)).start()
            return carry

        choose(z)
        pltpu.make_async_copy(send_b.at[z], b_place(z), b_sems.at[0]).start()
        lax.fori_loop(0, 7, send_b_to, 0)
        expect("b.send", send_b.at[pl.ds(0, 7)])

        need("f_own", "f1", "f2", "f3")
        for y_ in range(4):
            width = pl.ds(0, 128 * (y_ + 1))
            send(
                "f_x%d" % y_, fbuf.at[:, y_, xh, :, width], fbuf.at[:, y_, xh, :, width],
                2 * y + 1 - xh, col(z, 1 - xl, k), fbuf.at[:, y_, 1 - xh, :, width],
            )

        for d in (0, 1, 7, 2, 6, 3, 5, 4):
            place = b_place((z + 8 - d) % 8)
            wait_bytes(place, b_sems.at[d])
            for dy in (2, 1, 3):
                remote(place, place, sem("c.send"), sem("c"), 2 * ((y + dy) % 4) + xh, c).start()
        three = pbuf.at[:, :, :, pl.ds(0, 3)]
        expect("c", three)
        expect("c.send", three)
        pd_to, pd_x = z // 2, z % 2
        pd_self = jnp.logical_and(jnp.logical_or(pd_to == z, pd_to + 4 == z), xl == pd_x)

        def send_pd(j, carry):
            yd, t = (y + j // 2) % 4, j % 2
            for s in range(2):
                send_p[j, s] = buf_a[inv[s, 2 * (2 * yd + xh) + t], s]
            place = pdiag.at[:, xl, pl.ds(pl.multiple_of(8 * y, 8), 8), :]
            to_row, to_col = 2 * yd + xh, col(pd_to + 4 * t, pd_x, k)

            def away():
                remote(send_p.at[j], place, sem("pd.send"), sem("pd"), to_row, to_col).start()

            if isinstance(j, int):
                mine = to_col == c
                pl.when(mine)(lambda: pltpu.make_async_copy(send_p.at[j], place, sem("pd")).start())
                pl.when(jnp.logical_not(mine))(away)
            else:
                away()
            return carry

        lax.fori_loop(2, 8, send_pd, 0)
        send_pd(0, 0)
        send_pd(1, 0)
        expect("pd", pdiag)

        def wait_send_pd():
            pl.when(pd_self)(lambda: wait_bytes(send_p.at[pl.ds(0, 7)], sem("pd.send")))
            pl.when(jnp.logical_not(pd_self))(lambda: wait_bytes(send_p, sem("pd.send")))

        pending["pd.send"] = wait_send_pd


        need("anc")
        for s in range(2):
            for j in range(4):
                high, low = halves(abuf[s, j])
                a_high[s, :, 128 * j : 128 * j + 128] = high
                a_low[s, :, 128 * j : 128 * j + 128] = low

        need("c")

        ways = ((1, pl.ds(0, 128)), (7, pl.ds(128, 128)))
        xs = ((xl + 1) % 2, xl)
        def product(s, places):
            rows = [pl.ds(pl.multiple_of(64 * zd, 64), 64) for zd in places]
            left_high = jnp.concatenate([a_high[s, some, :] for some in rows], axis=0)
            left_low = jnp.concatenate([a_low[s, some, :] for some in rows], axis=0)
            sums = dot3(left_high, left_low, p_high[s], p_low[s])
            for n, zd in enumerate(places):
                cbuf[s, pl.ds(2 * zd, 2)] = sums[64 * n : 64 * n + 64].reshape(2, 32, 256)

        for s in range(2):
            high, low = halves(pbuf[s].reshape(512, 256))
            p_high[s] = high
            p_low[s] = low
            product(s, [(z + d) % 8 for d in (4, 3, 5)])
            for i, xd in enumerate(xs):
                for w, (up, half) in enumerate(ways):
                    remote(
                        cbuf.at[s, 2 * ((z + 4) % 8) + xd, :, half], relay4.at[w, i, s],
                        sem("relay.send"), relay_sems.at[w, i, 0], r, col((z + 2 * up) % 8, xl, k),
                    ).start()
                    remote(
                        cbuf.at[s, 2 * ((z + 3 * up) % 8) + xd], relay3.at[w, i, s],
                        sem("relay.send"), relay_sems.at[w, i, 1], r, col((z + up) % 8, xl, k),
                    ).start()
        for s in range(2):
            product(s, [(z + d) % 8 for d in (1, 7, 2, 6, 0)])
        expect("relay.send", cbuf.at[:, pl.ds(0, 6)])

        def send_sum(zd, xd, slot):
            remote(
                cbuf.at[:, 2 * zd + xd], rbuf.at[xl, slot], sem("sum.send"), sem("sum"), r, col(zd, xd, k)
            ).start()

        for xd in xs:
            for w, (up, half) in enumerate(ways):
                send_sum((z + up) % 8, xd, 1 + w)
        send_sum(z, 1 - xl, 0)
        rbuf[xl, 0] = cbuf[:, q]
        expect("sum", cbuf.at[:, pl.ds(0, 9)])
        expect("sum.send", cbuf.at[:, pl.ds(0, 9)])

        for i, xd in enumerate(xs):
            for w, (up, half) in enumerate(ways):
                wait_bytes(relay4.at[w, i], relay_sems.at[w, i, 0])
                wait_bytes(relay3.at[w, i], relay_sems.at[w, i, 1])
                zd = (z + 2 * up) % 8
                for s in range(2):
                    cbuf[s, 2 * zd + xd] += relay3[w, i, s]
                    cbuf[s, 2 * zd + xd, :, half] += relay4[w, i, s]
                send_sum(zd, xd, 3 + w)

        need("f_x0", "f_x1", "f_x2", "f_x3")
        own_rows = fbuf[:, y, xh]
        own_sq[...] = jnp.sum(own_rows * own_rows, axis=1)
        need("pd")
        for s in range(2):
            for y_ in range(4):
                rows, width = slice(128 * y_, 128 * y_ + 128), 128 * (y_ + 1)
                high, low = halves(fbuf[s, y_, :, :, :width].reshape(128, width))
                f_high[s, rows, :width] = high
                f_low[s, rows, :width] = low
                if y_ % 2 == 0:
                    f_high[s, rows, width : width + 128] = jnp.zeros((128, 128), BF16)
                    f_low[s, rows, width : width + 128] = jnp.zeros((128, 128), BF16)
            spread[s] = times_factor(
                jnp.concatenate([pdiag[s, 0], pdiag[s, 1]], axis=1), f_high.at[s], f_low.at[s]
            )
        need("sum")

        for s in range(2):
            total = jnp.concatenate([jnp.sum(rbuf[0, :, s], axis=0), jnp.sum(rbuf[1, :, s], axis=0)], axis=1)
            result = times_factor(total, f_high.at[s], f_low.at[s])
            d_send[s : s + 1, :] = jnp.sum(spread[s] * result, axis=0, keepdims=True)
            prod[:, s] = -result.reshape(2, 16, 512)

        for dz in (4, 3, 5, 2, 6, 1, 7, 0):
            for xd in (1 - xl, xl):
                if dz or xd is not xl:
                    remote(d_send, d1.at[q], sem("d1.send"), sem("d1"), r, col((z + dz) % 8, xd, k)).start()
        expect("d1", d1.at[pl.ds(0, 15)])
        expect("d1.send", d1.at[pl.ds(0, 15)])
        d1[q] = d_send[...]
        send("o", prod.at[0], out_block, r, c - 1, None)
        out_block[...] = prod[1]
        need("d1")
        d1_sum[...] = jnp.sum(d1[...], axis=0) + own_sq[...]
        for dy, flip in ((2, 1), (1, 1), (3, 1), (2, 0), (0, 1), (1, 0), (3, 0), (0, 0)):
            to = 2 * ((y + dy) % 4) + (xh + flip) % 2
            remote(d1_sum, d2.at[r], sem("d2.send"), sem("d2"), to, c - 1).start()
            if dy or flip:
                remote(d1_sum, d2.at[r], sem("d2.send"), sem("d2"), to, c).start()
        d2[r] = d1_sum[...]
        expect("d2", d1.at[pl.ds(0, 7)])
        expect("d2.send", d1.at[pl.ds(0, 15)])
        need("d2")
        out_diag[...] = jnp.sum(d2[...], axis=0)

    @pl.when(k == 1)
    def _():
        body()
        need(*pending)


def per_device(ancestor, panel, factor_inv, pattern):
    vmem = pltpu.VMEM
    inputs = [pltpu.with_memory_space_constraint(x, pltpu.HBM) for x in (ancestor, panel, factor_inv, pattern)]
    return pl.pallas_call(
        kernel,
        out_shape=(jax.ShapeDtypeStruct((2, 16, 512), F32), jax.ShapeDtypeStruct((2, 512), F32)),
        in_specs=[pl.BlockSpec(memory_space=pl.ANY)] * 4,
        out_specs=(pl.BlockSpec(memory_space=vmem), pl.BlockSpec(memory_space=vmem)),
        scratch_shapes=[
            pltpu.SMEM((2, 16), jnp.int32),
            pltpu.SMEM((2, 16), jnp.int32),
            vmem((16, 2, 8, 256), F32),
            vmem((8, 2, 2, 8, 256), F32),
            vmem((8, 2, 8, 256), F32),
            vmem((2, 2, 8, 4, 8, 256), F32),
            vmem((2, 4, 512, 128), F32),
            vmem((2, 4, 2, 64, 512), F32),
            vmem((2, 16, 32, 256), F32),
            vmem((2, 5, 2, 32, 256), F32),
            vmem((2, 2, 2, 32, 256), F32),
            vmem((2, 2, 2, 32, 128), F32),
            vmem((2, 2, 32, 256), F32),
            vmem((2, 32, 512), F32),
            vmem((2, 2, 16, 512), F32),
            vmem((2, 512), F32),
            vmem((2, 512), F32),
            vmem((16, 2, 512), F32),
            vmem((2, 512), F32),
            vmem((8, 2, 512), F32),
            vmem((2, 512, 512), BF16),
            vmem((2, 512, 512), BF16),
            vmem((2, 512, 256), BF16),
            vmem((2, 512, 256), BF16),
            vmem((2, 512, 512), BF16),
            vmem((2, 512, 512), BF16),
            pltpu.SemaphoreType.DMA((40,)),
            pltpu.SemaphoreType.DMA((8,)),
            pltpu.SemaphoreType.DMA((2, 2, 2)),
        ],
        compiler_params=pltpu.CompilerParams(
            collective_id=0, has_side_effects=True, vmem_limit_bytes=32 * 1024 * 1024
        ),
    )(*inputs)


def solution(mesh):
    in_specs = (P(None, "row", "col"), P(None, "col", None), P(None, "row", None), P())
    out_specs = (P(None, ("row", "col"), None), P())
    return jax.shard_map(per_device, mesh=mesh, in_specs=in_specs, out_specs=out_specs, check_vma=False)
```

```python
import jax
import jax.numpy as jnp
from jax import lax
from jax.experimental import pallas as pl
from jax.experimental.pallas import tpu as pltpu
from jax.sharding import PartitionSpec as P


MESH = pl.DeviceIdType.MESH
F32 = jnp.float32
BF16 = jnp.bfloat16


def halves(x):
    high = x.astype(BF16)
    low = (x - high.astype(F32)).astype(BF16)
    return high, low


def dot3(a_high, a_low, b_high, b_low):
    def dot(a, b):
        return jnp.dot(a, b, preferred_element_type=F32)

    return dot(a_high, b_high) + (dot(a_low, b_high) + dot(a_high, b_low))


def times_factor(x, f_high, f_low):
    high, low = halves(x)
    both = jnp.concatenate([high, low], axis=0)
    n = x.shape[0]

    def part(first, cols):
        rows = slice(first, 512)
        twice = jnp.dot(both[:, rows], f_high[rows, cols], preferred_element_type=F32)
        return twice[:n] + (twice[n:] + jnp.dot(high[:, rows], f_low[rows, cols], preferred_element_type=F32))

    return jnp.concatenate([part(0, slice(0, 256)), part(256, slice(256, 512))], axis=1)


def kernel(
    anc, pan, fin, pat_hbm, out_block, out_diag,
    pat, inv, buf_a, send_b, send_p, pbuf, abuf, fbuf, cbuf, rbuf, relay3, relay4, pdiag, spread, prod, d_send, own_sq,
    d1, d1_sum, d2, a_high, a_low, p_high, p_low, f_high, f_low, sems, b_sems, relay_sems,
):
    r = lax.axis_index("row")
    c = lax.axis_index("col")
    y, xh = r // 2, r % 2
    z, xl, k = c // 4, (c // 2) % 2, c % 2
    q = 2 * z + xl

    names = {}
    pending = {}

    def sem(name):
        return sems.at[names.setdefault(name, len(names))]

    def col(z_, xl_, k_):
        return z_ * 4 + xl_ * 2 + k_

    def remote(src, dst, send_sem, recv_sem, row_, col_):
        return pltpu.make_async_remote_copy(
            src_ref=src, dst_ref=dst, send_sem=send_sem, recv_sem=recv_sem, device_id=(row_, col_), device_id_type=MESH
        )

    def wait_bytes(ref, s):
        pltpu.make_async_copy(ref, ref, s).wait()

    def expect(name, ref):
        pending[name] = lambda: wait_bytes(ref, sem(name))

    def need(*keys):
        for key in keys:
            pending.pop(key)()

    def send(name, src, dst, row_, col_, arrives):
        copy = remote(src, dst, sem(name + ".send"), sem(name), row_, col_)
        copy.start()
        pending[name + ".send"] = copy.wait_send
        if arrives is not None:
            expect(name, arrives)

    barrier = pltpu.get_barrier_semaphore()

    def greet(row_, col_):
        pl.semaphore_signal(barrier, inc=1, device_id=(row_, col_), device_id_type=MESH)

    def piece(zi, xi):
        return pan.at[:, pl.ds(pl.multiple_of(32 * (zi % 4) + 8 * y, 8), 8), pl.ds(pl.multiple_of(256 * xi, 256), 256)]

    quarter = abuf.at[:, 2 * xl + k]

    @pl.when(k == 0)
    def _():
        def greet_row(j, carry):
            greet((r + j) % 8, c + 1)
            return carry

        lax.fori_loop(0, 8, greet_row, 0)
        pl.semaphore_wait(barrier, 16)

        def send_a(j, carry):
            zi, xi = (z + 3 - j // 2) % 4, (xl + j + 1) % 2
            remote(piece(zi, xi), buf_a.at[q], sem("a.send"), sem("a"), r, col(zi, xi, 1)).start()
            return carry

        lax.fori_loop(0, 8, send_a, 0)
        anc_x = remote(anc, quarter, sem("anc_x"), sem("anc"), r, col(z, 1 - xl, 1))
        anc_x.start()
        anc_core = remote(anc, quarter, sem("anc_core"), sem("anc"), r, c + 1)
        anc_core.start()
        wait_bytes(buf_a.at[pl.ds(0, 8)], sem("a.send"))
        anc_x.wait_send()
        anc_core.wait_send()
        wait_bytes(out_block, sem("o"))
        wait_bytes(d2, sem("d2"))
        out_diag[...] = jnp.sum(d2[...], axis=0)

    def body():
        pat_copy = pltpu.make_async_copy(pat_hbm, pat, sem("pat"))
        pat_copy.start()
        pending["pat"] = pat_copy.wait

        def greet_col(j, carry):
            half = j // 2
            other = (c + 16 + jnp.where(j % 2 == 0, half, 32 - half)) % 32
            greet(r, other)
            return carry

        lax.fori_loop(1, 32, greet_col, 0)
        for d in (2, 1, 3):
            greet(2 * ((y + d) % 4) + xh, c)
        greet(2 * y + 1 - xh, col(z, 1 - xl, k))
        pl.semaphore_wait(barrier, 15 + 3 + 1 + 8)

        def send_a(j, carry):
            zi, xi = 4 + (z + j // 2) % 4, (xl + j) % 2
            remote(piece(zi, xi), buf_a.at[q], sem("a.send"), sem("a"), r, col(zi, xi, 1)).start()
            return carry

        lax.fori_loop(1, 8, send_a, 0)

        @pl.when(z >= 4)
        def _():
            pltpu.make_async_copy(piece(z, xl), buf_a.at[q], sem("a")).start()

        @pl.when(z < 4)
        def _():
            remote(piece(4 + z, xl), buf_a.at[q], sem("a.send"), sem("a"), r, col(4 + z, xl, 1)).start()

        expect("a", buf_a)

        def wait_send_a():
            pl.when(z >= 4)(lambda: wait_bytes(buf_a.at[pl.ds(0, 7)], sem("a.send")))
            pl.when(z < 4)(lambda: wait_bytes(buf_a.at[pl.ds(0, 8)], sem("a.send")))

        pending["a.send"] = wait_send_a

        own = fbuf.at[:, y, xh]
        f_own = pltpu.make_async_copy(fin, own, sem("f_own"))
        f_own.start()
        pending["f_own"] = f_own.wait
        for d in (2, 1, 3):
            send("f%d" % d, fin, own, 2 * ((y + d) % 4) + xh, c, fbuf.at[:, (y + 4 - d) % 4, xh])

        pltpu.make_async_copy(anc, quarter, sem("anc")).start()
        anc_x = remote(anc, quarter, sem("anc_x"), sem("anc"), r, col(z, 1 - xl, 1))
        anc_x.start()
        pending["anc_x"] = anc_x.wait_send
        expect("anc", abuf)

        need("pat")

        def invert(n, carry):
            for s in range(2):
                found = jnp.int32(0)
                for j in range(16):
                    found = jnp.where(pat[s, j] == n, jnp.int32(j), found)
                inv[s, n] = found
            return carry

        lax.fori_loop(0, 16, invert, 0)
        need("a")

        def b_place(zi):
            return pbuf.at[:, :, zi, y]

        def choose(zd):
            for s in range(2):
                for t in range(2):
                    send_b[zd, s, t] = buf_a[inv[s, 2 * zd + t], s]

        def near_first(j):
            half = j // 2 + 1
            return jnp.where(j % 2 == 0, half, 8 - half)

        def send_b_to(j, carry):
            d = near_first(j)
            zd = (z + d) % 8
            choose(zd)
            remote(send_b.at[zd], b_place(z), sem("b.send"), b_sems.at[d], r, col(zd, xl, k)).start()
            return carry

        choose(z)
        pltpu.make_async_copy(send_b.at[z], b_place(z), b_sems.at[0]).start()
        lax.fori_loop(0, 7, send_b_to, 0)
        expect("b.send", send_b.at[pl.ds(0, 7)])

        need("f_own", "f1", "f2", "f3")
        for y_ in range(4):
            width = pl.ds(0, 128 * (y_ + 1))
            send(
                "f_x%d" % y_, fbuf.at[:, y_, xh, :, width], fbuf.at[:, y_, xh, :, width],
                2 * y + 1 - xh, col(z, 1 - xl, k), fbuf.at[:, y_, 1 - xh, :, width],
            )

        for d in (0, 1, 7, 2, 6, 3, 5, 4):
            place = b_place((z + 8 - d) % 8)
            wait_bytes(place, b_sems.at[d])
            for dy in (2, 1, 3):
                remote(place, place, sem("c.send"), sem("c"), 2 * ((y + dy) % 4) + xh, c).start()
        three = pbuf.at[:, :, :, pl.ds(0, 3)]
        expect("c", three)
        expect("c.send", three)
        pd_to, pd_x = z // 2, z % 2
        pd_self = jnp.logical_and(jnp.logical_or(pd_to == z, pd_to + 4 == z), xl == pd_x)

        def send_pd(j, carry):
            yd, t = (y + j // 2) % 4, j % 2
            for s in range(2):
                send_p[j, s] = buf_a[inv[s, 2 * (2 * yd + xh) + t], s]
            place = pdiag.at[:, xl, pl.ds(pl.multiple_of(8 * y, 8), 8), :]
            to_row, to_col = 2 * yd + xh, col(pd_to + 4 * t, pd_x, k)

            def away():
                remote(send_p.at[j], place, sem("pd.send"), sem("pd"), to_row, to_col).start()

            if isinstance(j, int):
                mine = to_col == c
                pl.when(mine)(lambda: pltpu.make_async_copy(send_p.at[j], place, sem("pd")).start())
                pl.when(jnp.logical_not(mine))(away)
            else:
                away()
            return carry

        lax.fori_loop(2, 8, send_pd, 0)
        send_pd(0, 0)
        send_pd(1, 0)
        expect("pd", pdiag)

        def wait_send_pd():
            pl.when(pd_self)(lambda: wait_bytes(send_p.at[pl.ds(0, 7)], sem("pd.send")))
            pl.when(jnp.logical_not(pd_self))(lambda: wait_bytes(send_p, sem("pd.send")))

        pending["pd.send"] = wait_send_pd


        need("anc")
        for s in range(2):
            for j in range(4):
                high, low = halves(abuf[s, j])
                a_high[s, :, 128 * j : 128 * j + 128] = high
                a_low[s, :, 128 * j : 128 * j + 128] = low

        need("c")

        ways = ((1, pl.ds(0, 128)), (7, pl.ds(128, 128)))
        xs = ((xl + 1) % 2, xl)
        def product(s, places):
            rows = [pl.ds(pl.multiple_of(64 * zd, 64), 64) for zd in places]
            left_high = jnp.concatenate([a_high[s, some, :] for some in rows], axis=0)
            left_low = jnp.concatenate([a_low[s, some, :] for some in rows], axis=0)
            sums = dot3(left_high, left_low, p_high[s], p_low[s])
            for n, zd in enumerate(places):
                cbuf[s, pl.ds(2 * zd, 2)] = sums[64 * n : 64 * n + 64].reshape(2, 32, 256)

        for s in range(2):
            high, low = halves(pbuf[s].reshape(512, 256))
            p_high[s] = high
            p_low[s] = low
            product(s, [(z + d) % 8 for d in (4, 3, 5)])
            for i, xd in enumerate(xs):
                for w, (up, half) in enumerate(ways):
                    remote(
                        cbuf.at[s, 2 * ((z + 4) % 8) + xd, :, half], relay4.at[w, i, s],
                        sem("relay.send"), relay_sems.at[w, i, 0], r, col((z + 2 * up) % 8, xl, k),
                    ).start()
                    remote(
                        cbuf.at[s, 2 * ((z + 3 * up) % 8) + xd], relay3.at[w, i, s],
                        sem("relay.send"), relay_sems.at[w, i, 1], r, col((z + up) % 8, xl, k),
                    ).start()
        for s in range(2):
            product(s, [(z + d) % 8 for d in (1, 7, 2, 6, 0)])
        expect("relay.send", cbuf.at[:, pl.ds(0, 6)])

        def send_sum(zd, xd, slot):
            remote(
                cbuf.at[:, 2 * zd + xd], rbuf.at[xl, slot], sem("sum.send"), sem("sum"), r, col(zd, xd, k)
            ).start()

        for xd in xs:
            for w, (up, half) in enumerate(ways):
                send_sum((z + up) % 8, xd, 1 + w)
        send_sum(z, 1 - xl, 0)
        rbuf[xl, 0] = cbuf[:, q]
        expect("sum", cbuf.at[:, pl.ds(0, 9)])
        expect("sum.send", cbuf.at[:, pl.ds(0, 9)])

        for i, xd in enumerate(xs):
            for w, (up, half) in enumerate(ways):
                wait_bytes(relay4.at[w, i], relay_sems.at[w, i, 0])
                wait_bytes(relay3.at[w, i], relay_sems.at[w, i, 1])
                zd = (z + 2 * up) % 8
                for s in range(2):
                    cbuf[s, 2 * zd + xd] += relay3[w, i, s]
                    cbuf[s, 2 * zd + xd, :, half] += relay4[w, i, s]
                send_sum(zd, xd, 3 + w)

        need("f_x0", "f_x1", "f_x2", "f_x3")
        own_rows = fbuf[:, y, xh]
        own_sq[...] = jnp.sum(own_rows * own_rows, axis=1)
        need("pd")
        for s in range(2):
            for y_ in range(4):
                rows, width = slice(128 * y_, 128 * y_ + 128), 128 * (y_ + 1)
                high, low = halves(fbuf[s, y_, :, :, :width].reshape(128, width))
                f_high[s, rows, :width] = high
                f_low[s, rows, :width] = low
                if y_ % 2 == 0:
                    f_high[s, rows, width : width + 128] = jnp.zeros((128, 128), BF16)
                    f_low[s, rows, width : width + 128] = jnp.zeros((128, 128), BF16)
            spread[s] = times_factor(
                jnp.concatenate([pdiag[s, 0], pdiag[s, 1]], axis=1), f_high.at[s], f_low.at[s]
            )
        need("sum")

        results = []
        for s in range(2):
            total = jnp.concatenate([jnp.sum(rbuf[0, :, s], axis=0), jnp.sum(rbuf[1, :, s], axis=0)], axis=1)
            result = times_factor(total, f_high.at[s], f_low.at[s])
            d_send[s : s + 1, :] = jnp.sum(spread[s] * result, axis=0, keepdims=True)
            results.append(result)

        for dz in (4, 3, 5, 2, 6, 1, 7, 0):
            for xd in (1 - xl, xl):
                if dz or xd is not xl:
                    remote(d_send, d1.at[q], sem("d1.send"), sem("d1"), r, col((z + dz) % 8, xd, k)).start()
        expect("d1", d1.at[pl.ds(0, 15)])
        expect("d1.send", d1.at[pl.ds(0, 15)])
        d1[q] = d_send[...]
        for s in range(2):
            prod[:, s] = -results[s].reshape(2, 16, 512)
        send("o", prod.at[0], out_block, r, c - 1, None)
        out_block[...] = prod[1]
        need("d1")
        d1_sum[...] = jnp.sum(d1[...], axis=0) + own_sq[...]
        for dy, flip in ((2, 1), (1, 1), (3, 1), (2, 0), (0, 1), (1, 0), (3, 0), (0, 0)):
            to = 2 * ((y + dy) % 4) + (xh + flip) % 2
            remote(d1_sum, d2.at[r], sem("d2.send"), sem("d2"), to, c - 1).start()
            if dy or flip:
                remote(d1_sum, d2.at[r], sem("d2.send"), sem("d2"), to, c).start()
        d2[r] = d1_sum[...]
        expect("d2", d1.at[pl.ds(0, 7)])
        expect("d2.send", d1.at[pl.ds(0, 15)])
        need("d2")
        out_diag[...] = jnp.sum(d2[...], axis=0)

    @pl.when(k == 1)
    def _():
        body()
        need(*pending)


def per_device(ancestor, panel, factor_inv, pattern):
    vmem = pltpu.VMEM
    inputs = [pltpu.with_memory_space_constraint(x, pltpu.HBM) for x in (ancestor, panel, factor_inv, pattern)]
    return pl.pallas_call(
        kernel,
        out_shape=(jax.ShapeDtypeStruct((2, 16, 512), F32), jax.ShapeDtypeStruct((2, 512), F32)),
        in_specs=[pl.BlockSpec(memory_space=pl.ANY)] * 4,
        out_specs=(pl.BlockSpec(memory_space=vmem), pl.BlockSpec(memory_space=vmem)),
        scratch_shapes=[
            pltpu.SMEM((2, 16), jnp.int32),
            pltpu.SMEM((2, 16), jnp.int32),
            vmem((16, 2, 8, 256), F32),
            vmem((8, 2, 2, 8, 256), F32),
            vmem((8, 2, 8, 256), F32),
            vmem((2, 2, 8, 4, 8, 256), F32),
            vmem((2, 4, 512, 128), F32),
            vmem((2, 4, 2, 64, 512), F32),
            vmem((2, 16, 32, 256), F32),
            vmem((2, 5, 2, 32, 256), F32),
            vmem((2, 2, 2, 32, 256), F32),
            vmem((2, 2, 2, 32, 128), F32),
            vmem((2, 2, 32, 256), F32),
            vmem((2, 32, 512), F32),
            vmem((2, 2, 16, 512), F32),
            vmem((2, 512), F32),
            vmem((2, 512), F32),
            vmem((16, 2, 512), F32),
            vmem((2, 512), F32),
            vmem((8, 2, 512), F32),
            vmem((2, 512, 512), BF16),
            vmem((2, 512, 512), BF16),
            vmem((2, 512, 256), BF16),
            vmem((2, 512, 256), BF16),
            vmem((2, 512, 512), BF16),
            vmem((2, 512, 512), BF16),
            pltpu.SemaphoreType.DMA((40,)),
            pltpu.SemaphoreType.DMA((8,)),
            pltpu.SemaphoreType.DMA((2, 2, 2)),
        ],
        compiler_params=pltpu.CompilerParams(
            collective_id=0, has_side_effects=True, vmem_limit_bytes=32 * 1024 * 1024
        ),
    )(*inputs)


def solution(mesh):
    in_specs = (P(None, "row", "col"), P(None, "col", None), P(None, "row", None), P())
    out_specs = (P(None, ("row", "col"), None), P())
    return jax.shard_map(per_device, mesh=mesh, in_specs=in_specs, out_specs=out_specs, check_vma=False)
```
